32 devices in a mesh: tm: 4 (over y, core), vert: 8 (over z, x).
Axes of the slice: x: 2, y: 2, z: 4, core: 2. Of those that a mesh axis runs over, the one named last changes fastest.
Arguments:
- features: bfloat16 [4, 4096, 1024], P('tm', 'vert'), may hold values from -6 to 6
- graph_weight: bfloat16 [1024, 1024], P('vert'), may hold values from -0.1875 to 0.1875
- head_weight: bfloat16 [16, 192, 1024], P('tm'), may hold values from -16 to 16
- send_rows: int32 [4, 8, 8, 16], P('tm', 'vert'), may hold values from 0 to 511, as said below
- send_count: int32 [4, 8, 8], P('tm', 'vert'), may hold values from 0 to 16, as said below
- block_index: int32 [4, 32, 3], P('tm', 'vert'), may hold values from 0 to 4, as said below
- block_values: bfloat16 [4, 4096, 3, 128], P('tm', 'vert'), may hold values from -0.3125 to 0.3125
Outputs:
- combined: bfloat16 [4, 4096, 1024], P('tm', 'vert')
The draws below stay inside these ranges and needn't reach their ends.
Inputs may be any that keep to these rules, and one draw needn't show every extreme that they name: send_rows[s, p, q] holds 16 distinct local rows of partition p; slots from send_count[s, p, q] on are ignored. send_count[s, p, p] is 0; in every snapshot some pairs reach 16. `block_index`: the 3 entries of a block row are distinct; column blocks below 4 are the partition's own rows, the others its boundary rows in the order of columns.
All inputs are finite; a program needn't handle non-finite values.
Results may differ from the reference program's by a relative error of at most 0.0075.
Values may be sent and summed in bfloat16 or wider, within the bound.
No kernel may reach another device: no remote copies, remote signals or barrier semaphores. Data moves between devices by JAX's collectives and lax.ppermute only.
A program may use at most 64 MiB of HBM per device.

```python
import jax
import jax.numpy as jnp
from jax import lax

D = 1024
HEADS = 16
HS = 64
BLK = 128
NBLK = 3
BMAX = 16
V_DEV = 512
SNAPS = 4
NPART = 8
VERTS = 4096
LB = 4
CB = 5


def draw_head_weight(key, part):
    scale = D ** (-0.5)
    base = jax.random.normal(jax.random.fold_in(key, 11), (HEADS, 3 * HS, D), jnp.float32) * scale
    base = jnp.clip(base, -6.0 * scale, 6.0 * scale)
    return base.astype(jnp.bfloat16)


def draw_send_rows(key, part):
    keys_all = jax.random.split(jax.random.fold_in(key, 21), SNAPS * NPART * NPART)
    rows_all = jax.vmap(lambda single: jax.random.permutation(single, V_DEV)[:BMAX])(keys_all)
    return rows_all.reshape(SNAPS, NPART, NPART, BMAX).astype(jnp.int32)


def draw_send_count(key, part):
    level = jax.random.randint(jax.random.fold_in(key, 31), (SNAPS, 1, NPART), 1, 5)
    base = jax.random.randint(jax.random.fold_in(key, 32), (SNAPS, NPART, NPART), 0, (BMAX + 3) // 4 + 1)
    counts = jnp.minimum(base * level, BMAX)
    source = jnp.arange(NPART)[:, None]
    target = jnp.arange(NPART)[None, :]
    counts = jnp.where((target == (source + 1) % NPART)[None], BMAX, counts)
    counts = jnp.where((target == source)[None], 0, counts)
    return counts.astype(jnp.int32)


def draw_block_index(key, part):
    keys_all = jax.random.split(jax.random.fold_in(key, 41), SNAPS * NPART * LB)
    picks = jax.vmap(lambda single: jax.random.permutation(single, CB)[:NBLK])(keys_all)
    return picks.reshape(SNAPS, NPART * LB, NBLK).astype(jnp.int32)


def block_levels(rng, shape, cuts, low, largest):
    def one(dim, blocks):
        steps = jax.random.uniform(jax.random.fold_in(jax.random.fold_in(rng, 6), dim), (blocks,), jnp.float32, low / len(cuts), largest / len(cuts))
        return jnp.repeat(jnp.exp(steps), shape[dim] // blocks).reshape((-1,) + (1,) * (len(shape) - dim - 1))

    loudness = one(*cuts[0])
    for cut in cuts[1:]:
        loudness = loudness * one(*cut)
    return loudness


def gaussian(rng, extent, deviation, limit, pieces=(), kind=jnp.bfloat16):
    drawn = jax.random.normal(rng, extent, jnp.float32) * deviation
    if len(pieces) > 0:
        drawn = block_levels(rng, extent, pieces, -0.22, 0.18) * drawn
    return jnp.clip(drawn, min=-limit, max=limit).astype(kind)


def setup_inputs(seed: int = 0) -> dict:
    key_list = jax.random.split(jax.random.key(seed), 8)
    return {
        "features": gaussian(key_list[0], (SNAPS, VERTS, D), 1.0, 6.0, ((0, 4), (1, 8))),
        "graph_weight": gaussian(key_list[1], (D, D), D ** -0.5, 0.1875, ((0, 8),)),
        "head_weight": draw_head_weight(jax.random.fold_in(key_list[7], 71), 0),
        "send_rows": draw_send_rows(jax.random.fold_in(key_list[7], 71), 0),
        "send_count": draw_send_count(jax.random.fold_in(key_list[7], 71), 0),
        "block_index": draw_block_index(jax.random.fold_in(key_list[7], 71), 0),
        "block_values": gaussian(key_list[6], (SNAPS, VERTS, NBLK, BLK), (NBLK * BLK) ** -0.5, 0.3125, ((0, 4), (1, 8))),
    }


def graph_snapshot(features_s, graph_weight, rows_s, count_s, index_s, values_s):
    projected = jnp.dot(features_s, graph_weight, preferred_element_type=jnp.float32).astype(jnp.bfloat16)
    projected_parts = projected.reshape(NPART, V_DEV, D)
    slot_ids = jnp.arange(BMAX, dtype=jnp.int32)

    def partition_step(part_id):
        rows_q = rows_s[:, part_id, :]
        count_q = count_s[:, part_id]
        picked = jax.vmap(lambda part_rows, row_ids: part_rows[row_ids])(projected_parts, rows_q)
        live_slots = slot_ids[None, :] < count_q[:, None]
        picked = jnp.where(live_slots[:, :, None], picked, jnp.zeros_like(picked))
        own_rows = lax.dynamic_index_in_dim(projected_parts, part_id, 0, keepdims=False)
        columns = jnp.concatenate([own_rows, picked.reshape(NPART * BMAX, D)], axis=0).reshape(CB, BLK, D)
        index_q = lax.dynamic_slice_in_dim(index_s, (part_id * LB).astype(jnp.int32), LB, 0)
        values_q = lax.dynamic_slice_in_dim(values_s, (part_id * V_DEV).astype(jnp.int32), V_DEV, 0)
        values_q = values_q.reshape(LB, BLK, NBLK, BLK)
        chosen = columns[index_q]
        summed = jnp.einsum("rikj,rkjd->rid", values_q.astype(jnp.float32), chosen.astype(jnp.float32))
        pre_act = own_rows.astype(jnp.float32) + summed.reshape(V_DEV, D)
        return jax.nn.relu(pre_act).astype(jnp.bfloat16)

    return lax.map(partition_step, jnp.arange(NPART, dtype=jnp.int32))


def attend_block(hidden_block, head_weight):
    packed = jnp.einsum("tvd,hcd->tvhc", hidden_block.astype(jnp.float32), head_weight.astype(jnp.float32))
    queries = packed[..., :HS].astype(jnp.bfloat16).astype(jnp.float32)
    keys_part = packed[..., HS:2 * HS].astype(jnp.bfloat16).astype(jnp.float32)
    values = packed[..., 2 * HS:].astype(jnp.bfloat16).astype(jnp.float32)
    scores = jnp.einsum("tvhc,svhc->vhts", queries, keys_part) * (HS ** -0.5)
    causal = jnp.arange(SNAPS)[:, None] >= jnp.arange(SNAPS)[None, :]
    scores = jnp.where(causal, scores, -1e30)
    row_max = jnp.max(scores, axis=-1, keepdims=True)
    exponent = jnp.where(causal, jnp.exp(scores - row_max), 0.0)
    attention = (exponent / jnp.sum(exponent, axis=-1, keepdims=True)).astype(jnp.bfloat16).astype(jnp.float32)
    attended = jnp.einsum("vhts,svhc->tvhc", attention, values)
    return attended.astype(jnp.bfloat16).reshape(SNAPS, V_DEV, D)


def reference(features, graph_weight, head_weight, send_rows, send_count, block_index, block_values):
    hidden = lax.map(
        lambda items: graph_snapshot(items[0], graph_weight, items[1], items[2], items[3], items[4]),
        (features, send_rows, send_count, block_index, block_values))
    attended = lax.map(lambda part_id: attend_block(hidden[:, part_id], head_weight),
                       jnp.arange(NPART, dtype=jnp.int32))
    attended = jnp.transpose(attended, (1, 0, 2, 3)).reshape(SNAPS, VERTS, D)
    hidden = hidden.reshape(SNAPS, VERTS, D)
    return (hidden.astype(jnp.float32) + attended.astype(jnp.float32)).astype(jnp.bfloat16)
```

```python
import functools

import jax
import jax.numpy as jnp
from jax import lax
from jax.experimental import pallas as pl
from jax.experimental.pallas import tpu as pltpu
from jax.sharding import PartitionSpec as P

CORES = 2
ROW_BLOCKS = 4
VMEM = pl.BlockSpec(memory_space=pltpu.VMEM)
SMEM = pl.BlockSpec(memory_space=pltpu.SMEM)
MASKED = -1e30


def call(kernel, outs, ins, flops=0, scratch=(), limit=24):
    moved = sum(a.size * a.dtype.itemsize for a in (*ins, *jax.tree.leaves(outs)))
    return pl.pallas_call(
        kernel,
        out_shape=outs,
        in_specs=[SMEM if a.dtype == jnp.int32 else VMEM for a in ins],
        out_specs=jax.tree.map(lambda _: VMEM, outs),
        scratch_shapes=scratch,
        compiler_params=pltpu.CompilerParams(vmem_limit_bytes=limit * 2**20),
        cost_estimate=pl.CostEstimate(flops=flops, bytes_accessed=moved, transcendentals=0),
    )(*ins)


def mix_kernel(index_ref, own_ref, arrived_ref, edge_ref, mixed_ref, columns_ref):
    own = own_ref.shape[0]
    block_rows, chosen = index_ref.shape
    size = own // block_rows
    columns_ref[:own, :] = own_ref[...]
    columns_ref[own:, :] = arrived_ref[...]
    for b in range(block_rows):
        rows = slice(b * size, (b + 1) * size)
        total = own_ref[rows, :].astype(jnp.float32)
        for k in range(chosen):
            start = pl.multiple_of(index_ref[b, k] * size, size)
            total += jnp.dot(
                edge_ref[rows, k * size : (k + 1) * size],
                columns_ref[pl.ds(start, size), :],
                preferred_element_type=jnp.float32,
            )
        mixed_ref[rows, :] = total.astype(mixed_ref.dtype)


def relu_dot(left, right):
    total = jnp.dot(left, right, preferred_element_type=jnp.float32)
    return jnp.maximum(total, 0.0).astype(jnp.bfloat16)


def assemble_kernel(place_ref, mine_ref, other_ref, mixed_ref, weight_ref, hidden_ref):
    pieces, depth, width = mine_ref.shape
    for half, ref in enumerate((mine_ref, other_ref)):
        column = pl.multiple_of(place_ref[pieces + half] * width, width)
        for i in range(pieces):
            row = pl.multiple_of(place_ref[i] * depth, depth)
            weight_ref[pl.ds(row, depth), pl.ds(column, width)] = ref[i]
    hidden_ref[...] = relu_dot(mixed_ref[...], weight_ref[...])


def hidden_kernel(mixed_ref, weight_ref, hidden_ref):
    hidden_ref[...] = relu_dot(mixed_ref[...], weight_ref[...])


def attend_kernel(slots, pieces, head_size, flag_ref, *refs):
    hidden_refs, weight_refs = refs[:slots], refs[slots : slots + pieces]
    mine_ref, other_ref, stacked_ref = refs[slots + pieces :]
    rows = hidden_refs[0].shape[0]
    for s in range(slots):
        stacked_ref[s * rows : (s + 1) * rows, :] = hidden_refs[s][...]
    width = weight_refs[0].shape[0] // 3
    contract = (((1,), (1,)), ((), ()))
    group = lambda axis: lax.broadcasted_iota(jnp.int32, (2 * width, width), axis) % width // head_size
    spread = (group(0) == group(1)).astype(jnp.bfloat16)
    for p in range(pieces):
        weight = weight_refs[p]
        queries = lax.dot_general(
            stacked_ref[: CORES * rows, :], weight[:width, :], contract,
            preferred_element_type=jnp.float32,
        ).astype(jnp.bfloat16).astype(jnp.float32)
        both = lax.dot_general(
            stacked_ref[...], weight[width:, :], contract, preferred_element_type=jnp.float32
        ).astype(jnp.bfloat16).astype(jnp.float32)
        for t, out_ref in enumerate((mine_ref, other_ref)):
            query = queries[t * rows : (t + 1) * rows]
            products = jnp.concatenate(
                [query * both[u * rows : (u + 1) * rows, :width] for u in range(slots)], axis=0
            )
            high = products.astype(jnp.bfloat16)
            low = (products - high.astype(jnp.float32)).astype(jnp.bfloat16)
            scores = jnp.dot(
                jnp.concatenate([high, low], axis=1), spread, preferred_element_type=jnp.float32
            ) * head_size ** (-0.5)
            parts = [
                jnp.where(flag_ref[t * slots + u] > 0, scores[u * rows : (u + 1) * rows], MASKED)
                for u in range(slots)
            ]
            top = functools.reduce(jnp.maximum, parts)
            parts = [jnp.exp(part - top) for part in parts]
            scale = 1.0 / functools.reduce(jnp.add, parts)
            total = jnp.zeros_like(top)
            for u in range(slots):
                share = (parts[u] * scale).astype(jnp.bfloat16).astype(jnp.float32)
                total += share * both[u * rows : (u + 1) * rows, width:]
            out_ref[:, p * width : (p + 1) * width] = total.astype(out_ref.dtype)


def combine_kernel(blocks, pieces, place_ref, hidden_ref, *refs):
    out_ref = refs[-1]
    width = refs[0].shape[1] // pieces
    lanes = width % 128 == 0
    for r in range(blocks):
        rows = refs[r].shape[0]
        here = slice(r * rows, (r + 1) * rows)
        whole = None if lanes else hidden_ref[here, :].astype(jnp.float32)
        for half in range(CORES):
            for p in range(pieces):
                start = place_ref[half * pieces + p] * width
                attended = refs[half * blocks + r][:, p * width : (p + 1) * width]
                if lanes:
                    column = pl.ds(pl.multiple_of(start, width), width)
                    total = hidden_ref[here, column].astype(jnp.float32) + attended.astype(jnp.float32)
                    out_ref[here, column] = total.astype(out_ref.dtype)
                else:
                    shape = (width, out_ref.shape[1])
                    spot = lax.broadcasted_iota(jnp.int32, shape, 0) + start
                    spot = (spot == lax.broadcasted_iota(jnp.int32, shape, 1)).astype(jnp.bfloat16)
                    whole += jnp.dot(attended, spot, preferred_element_type=jnp.float32)
        if not lanes:
            out_ref[here, :] = whole.astype(out_ref.dtype)


def shards(sizes, features, graph_weight, head_weight, send_rows, send_count, block_index, block_values):
    steps, parts = sizes["tm"], sizes["vert"]
    chips = steps // CORES
    step, part = lax.axis_index("tm"), lax.axis_index("vert")
    core, chip = step % CORES, step // CORES
    swap_core = lambda a: lax.ppermute(a, "tm", [(i, i ^ 1) for i in range(steps)])
    swap_part = lambda a: lax.ppermute(a, "vert", [(i, i ^ 1) for i in range(parts)])
    inputs = features[0]
    own, width = inputs.shape

    rows_list = send_rows[0, 0]
    sources, most_rows = rows_list.shape
    live = jnp.arange(most_rows)[None, :] < send_count[0, 0][:, None]
    chosen = (rows_list[:, :, None] == jnp.arange(own)) & live[:, :, None]
    picked = jnp.einsum(
        "qjv,vd->qjd", chosen.astype(jnp.bfloat16), inputs, preferred_element_type=jnp.float32
    ).astype(jnp.bfloat16)
    arrived = lax.all_to_all(picked, "vert", split_axis=0, concat_axis=0, tiled=True)

    heads, head_rows, _ = head_weight.shape
    head_size = head_rows // 3
    shares = 2 if heads % 2 == 0 and parts % 2 == 0 else 1
    ordered = head_weight.reshape(shares, heads // shares, 3, head_size, width)
    ordered = ordered.transpose(0, 2, 1, 3, 4).reshape(shares, -1, width)
    share = part % shares
    sent = lax.dynamic_index_in_dim(ordered, share, 0, keepdims=False)
    weights = [ordered[i] for i in range(shares)]
    spots = [(step, i) for i in range(shares)]
    for d in range(1, chips):
        fetched = lax.ppermute(sent, "tm", [(i, (i + CORES * d) % steps) for i in range(steps)])
        weights.append(fetched)
        spots.append(((step - CORES * d) % steps, share))
        if shares == 2:
            weights.append(swap_part(fetched))
            spots.append(((step - CORES * d) % steps, 1 - share))
    place = [s * shares + i for s, i in spots] + [(s ^ 1) * shares + i for s, i in spots]
    place = jnp.stack([jnp.asarray(i, jnp.int32) for i in place])

    depth = graph_weight.shape[0]
    half = width // CORES
    piece = lax.dynamic_slice(graph_weight, (0, core * half), (depth, half))
    pieces = [piece]
    for d in range(1, parts // 2):
        pieces.append(lax.ppermute(piece, "vert", [(i, (i + 2 * d) % parts) for i in range(parts)]))
    pieces = pieces + [swap_part(piece) for piece in pieces]
    origin = [(part - 2 * d) % parts for d in range(parts // 2)]
    origin = jnp.stack(origin + [i ^ 1 for i in origin] + [core, 1 - core]).astype(jnp.int32)
    mine = jnp.stack(pieces)
    other = swap_core(mine)

    edges = block_values[0].reshape(own, -1)
    boundary = arrived.reshape(sources * most_rows, width)
    mixed = call(
        mix_kernel,
        jax.ShapeDtypeStruct((own, width), jnp.bfloat16),
        (block_index[0], inputs, boundary, edges),
        flops=2 * edges.size * width,
        scratch=[pltpu.VMEM((own + sources * most_rows, width), jnp.bfloat16)],
    )
    blocks = ROW_BLOCKS
    rows = own // blocks
    lower = []
    for r in range(blocks):
        chunk = mixed[r * rows : (r + 1) * rows]
        lower.append([
            lax.ppermute(chunk, "tm", [(i, i + CORES * d) for i in range(steps - CORES * d)])
            for d in range(1, chips)
        ])
    weight, hidden = call(
        assemble_kernel,
        (
            jax.ShapeDtypeStruct((width, width), jnp.bfloat16),
            jax.ShapeDtypeStruct((own, width), jnp.bfloat16),
        ),
        (origin, mine, other, mixed),
        flops=2 * own * width * width,
    )
    sibling = swap_core(hidden)

    slots = CORES * chips
    flags = [jnp.bool_(True), core == 1, core == 0, jnp.bool_(True)]
    reach = [chip >= d for d in range(1, chips) for _ in range(CORES)]
    flags = jnp.stack([*flags[:2], *reach, *flags[2:], *reach]).astype(jnp.int32)
    kept, got = [], []
    group = len(weights) * weights[0].shape[0] // 3
    for r in range(blocks):
        here = slice(r * rows, (r + 1) * rows)
        slot_rows = [hidden[here], sibling[here]]
        for chunk in lower[r]:
            raised = call(
                hidden_kernel,
                jax.ShapeDtypeStruct((rows, width), jnp.bfloat16),
                (chunk, weight),
                flops=2 * rows * width * width,
            )
            slot_rows += [raised, swap_core(raised)]
        shape = jax.ShapeDtypeStruct((rows, group), jnp.bfloat16)
        keep, send = call(
            functools.partial(attend_kernel, slots, len(weights), head_size),
            (shape, shape),
            (flags, *slot_rows, *weights),
            flops=2 * slots * rows * width * 3 * group,
            scratch=[pltpu.VMEM((slots * rows, width), jnp.bfloat16)],
            limit=40,
        )
        kept.append(keep)
        got.append(swap_core(send))

    combined = call(
        functools.partial(combine_kernel, blocks, len(weights)),
        jax.ShapeDtypeStruct((own, width), jnp.bfloat16),
        (place, hidden, *kept, *got),
    )
    return combined[None]


def solution(mesh):
    return jax.shard_map(
        functools.partial(shards, dict(mesh.shape)),
        mesh=mesh,
        in_specs=(
            P("tm", "vert", None),
            P("vert", None),
            P("tm", None, None),
            P("tm", "vert", None, None),
            P("tm", "vert", None),
            P("tm", "vert", None),
            P("tm", "vert", None, None),
        ),
        out_specs=P("tm", "vert", None),
        check_vma=False,
    )
```

```python
import functools

import jax
import jax.numpy as jnp
from jax import lax
from jax.experimental import pallas as pl
from jax.experimental.pallas import tpu as pltpu
from jax.sharding import PartitionSpec as P

CORES = 2
ROW_BLOCKS = 4
VMEM = pl.BlockSpec(memory_space=pltpu.VMEM)
SMEM = pl.BlockSpec(memory_space=pltpu.SMEM)
MASKED = -1e30
LANES = 128
NT = (((1,), (1,)), ((), ()))


def call(kernel, outs, ins, specs=None, out_specs=None, flops=0, scratch=(), limit=24, aliases=None):
    moved = sum(a.size * a.dtype.itemsize for a in (*ins, *jax.tree.leaves(outs)))
    return pl.pallas_call(
        kernel,
        out_shape=outs,
        grid=(1,) if specs else (),
        in_specs=specs or [SMEM if a.dtype == jnp.int32 else VMEM for a in ins],
        out_specs=out_specs or jax.tree.map(lambda _: VMEM, outs),
        scratch_shapes=scratch,
        input_output_aliases=aliases or {},
        compiler_params=pltpu.CompilerParams(vmem_limit_bytes=limit * 2**20),
        cost_estimate=pl.CostEstimate(flops=flops, bytes_accessed=moved, transcendentals=0),
    )(*ins)


def shaped(*shape):
    return jax.ShapeDtypeStruct(shape, jnp.bfloat16)


def mix_kernel(index_ref, own_ref, arrived_ref, edge_ref, *refs):
    own = own_ref.shape[0]
    *chunk_refs, mixed_ref, columns_ref = refs
    block_rows, chosen = index_ref.shape
    size = own // block_rows
    columns_ref[:own, :] = own_ref[...]
    columns_ref[own:, :] = arrived_ref[...]
    for b in range(block_rows):
        rows = slice(b * size, (b + 1) * size)
        total = own_ref[rows, :].astype(jnp.float32)
        for k in range(chosen):
            start = pl.multiple_of(index_ref[b, k] * size, size)
            total += jnp.dot(
                edge_ref[rows, k * size : (k + 1) * size],
                columns_ref[pl.ds(start, size), :],
                preferred_element_type=jnp.float32,
            )
        mixed_ref[rows, :] = total.astype(mixed_ref.dtype)
    rows = own // len(chunk_refs)
    for r, chunk_ref in enumerate(chunk_refs):
        chunk_ref[...] = mixed_ref[r * rows : (r + 1) * rows, :]


def relu_dot(left, right):
    total = jnp.dot(left, right, preferred_element_type=jnp.float32)
    return jnp.maximum(total, 0.0).astype(jnp.bfloat16)


def assemble_kernel(place_ref, mine_ref, other_ref, mixed_ref, weight_ref, hidden_ref):
    pieces, depth, width = mine_ref.shape
    for half, ref in enumerate((mine_ref, other_ref)):
        column = pl.multiple_of(place_ref[pieces + half] * width, width)
        for i in range(pieces):
            row = pl.multiple_of(place_ref[i] * depth, depth)
            weight_ref[pl.ds(row, depth), pl.ds(column, width)] = ref[i]
    hidden_ref[...] = relu_dot(mixed_ref[...], weight_ref[...])


def own_kernel(lists, mine_ref, other_ref, *refs):
    weight_refs = refs[:lists]
    pair_ref, query_ref, both_ref, ask_ref, stacked_ref = refs[lists:]
    rows = mine_ref.shape[0]
    pieces, double, _ = pair_ref.shape
    width = double // 2
    head_size = weight_refs[0].shape[1] // 3
    i = 0
    for ref in weight_refs:
        for j in range(ref.shape[0]):
            piece, start = divmod(i * head_size, width)
            here = slice(start, start + head_size)
            ask_ref[piece, here, :] = ref[j, :head_size, :]
            pair_ref[piece, here, :] = ref[j, head_size : 2 * head_size, :]
            here = slice(width + start, width + start + head_size)
            pair_ref[piece, here, :] = ref[j, 2 * head_size :, :]
            i += 1
    stacked_ref[:rows, :] = mine_ref[...]
    stacked_ref[rows:, :] = other_ref[...]
    for p in range(pieces):
        for weight_ref, out_ref in ((ask_ref, query_ref), (pair_ref, both_ref)):
            packed = lax.dot_general(
                stacked_ref[...], weight_ref[p], NT, preferred_element_type=jnp.float32
            ).astype(jnp.bfloat16)
            out_ref[0, p] = packed[:rows]
            out_ref[1, p] = packed[rows:]


def attend_kernel(groups, head_size, flag_ref, weight_ref, *refs):
    pair_refs, query_refs, both_refs = refs[:groups], refs[groups : 2 * groups], refs[2 * groups : 3 * groups]
    *mixed_refs, mine_ref, other_ref, stacked_ref = refs[3 * groups :]
    rows = mine_ref.shape[0]
    slots = CORES + len(mixed_refs)
    for s, ref in enumerate(mixed_refs):
        stacked_ref[s * rows : (s + 1) * rows, :] = ref[...]
    raised = relu_dot(stacked_ref[...], weight_ref[...])
    at = 0
    for pair_ref, query_ref, both_ref in zip(pair_refs, query_refs, both_refs):
        pieces, double, _ = pair_ref.shape
        width = double // 2
        group = lambda axis: lax.broadcasted_iota(jnp.int32, (double, width), axis) % width // head_size
        spread = (group(0) == group(1)).astype(jnp.bfloat16)
        for p in range(pieces):
            packed = lax.dot_general(
                raised, pair_ref[p], NT, preferred_element_type=jnp.float32
            ).astype(jnp.bfloat16)
            both = [both_ref[u, p].astype(jnp.float32) for u in range(CORES)]
            both += [
                packed[s * rows : (s + 1) * rows].astype(jnp.float32) for s in range(len(mixed_refs))
            ]
            for t, out_ref in enumerate((mine_ref, other_ref)):
                query = query_ref[t, p].astype(jnp.float32)
                products = jnp.concatenate([query * b[:, :width] for b in both], axis=0)
                high = products.astype(jnp.bfloat16)
                low = (products - high.astype(jnp.float32)).astype(jnp.bfloat16)
                scores = jnp.dot(
                    jnp.concatenate([high, low], axis=1), spread, preferred_element_type=jnp.float32
                ) * head_size ** (-0.5)
                parts = [
                    jnp.where(flag_ref[t * slots + u] > 0, scores[u * rows : (u + 1) * rows], MASKED)
                    for u in range(slots)
                ]
                top = functools.reduce(jnp.maximum, parts)
                parts = [jnp.exp(part - top) for part in parts]
                scale = 1.0 / functools.reduce(jnp.add, parts)
                total = jnp.zeros_like(top)
                for u in range(slots):
                    share = (parts[u] * scale).astype(jnp.bfloat16).astype(jnp.float32)
                    total += share * both[u][:, width:]
                out_ref[:, at : at + width] = total.astype(out_ref.dtype)
            at += width


def combine_kernel(pieces, place_ref, hidden_ref, mine_ref, other_ref, *refs):
    out_ref = refs[-1]
    width = mine_ref.shape[1] // pieces
    lanes = width % LANES == 0
    whole = None if lanes else hidden_ref[...].astype(jnp.float32)
    for half, attended_ref in enumerate((mine_ref, other_ref)):
        for p in range(pieces):
            start = place_ref[half * pieces + p] * width
            attended = attended_ref[:, p * width : (p + 1) * width]
            if lanes:
                column = pl.ds(pl.multiple_of(start, width), width)
                total = hidden_ref[:, column].astype(jnp.float32) + attended.astype(jnp.float32)
                out_ref[:, column] = total.astype(out_ref.dtype)
            else:
                shape = (width, out_ref.shape[1])
                spot = lax.broadcasted_iota(jnp.int32, shape, 0) + start
                spot = (spot == lax.broadcasted_iota(jnp.int32, shape, 1)).astype(jnp.bfloat16)
                whole += jnp.dot(attended, spot, preferred_element_type=jnp.float32)
    if not lanes:
        out_ref[...] = whole.astype(out_ref.dtype)


def shards(sizes, features, graph_weight, head_weight, send_rows, send_count, block_index, block_values):
    steps, parts = sizes["tm"], sizes["vert"]
    chips = steps // CORES
    step, part = lax.axis_index("tm"), lax.axis_index("vert")
    core, chip = step % CORES, step // CORES
    swap_core = lambda a: lax.ppermute(a, "tm", [(i, i ^ 1) for i in range(steps)])
    swap_part = lambda a, bit: lax.ppermute(a, "vert", [(i, i ^ bit) for i in range(parts)])
    inputs = features[0]
    own, width = inputs.shape

    heads, head_rows, _ = head_weight.shape
    head_size = head_rows // 3
    shared = heads % 4 == 0 and parts % 4 == 0
    shares = 2 if shared else 1
    share = (part ^ (part >> 1)) % shares
    sent = lax.dynamic_slice_in_dim(head_weight, share * (heads // shares), heads // shares, 0)
    fetched = [
        lax.ppermute(sent, "tm", [(i, (i + CORES * d) % steps) for i in range(steps)])
        for d in range(1, chips)
    ]

    rows_list = send_rows[0, 0]
    sources, most_rows = rows_list.shape
    live = jnp.arange(most_rows)[None, :] < send_count[0, 0][:, None]
    chosen = (rows_list[:, :, None] == jnp.arange(own)) & live[:, :, None]
    picked = jnp.einsum(
        "qjv,vd->qjd", chosen.astype(jnp.bfloat16), inputs, preferred_element_type=jnp.float32
    ).astype(jnp.bfloat16)
    arrived = lax.all_to_all(picked, "vert", split_axis=0, concat_axis=0, tiled=True)

    depth = graph_weight.shape[0]
    half = width // CORES
    piece = lax.dynamic_slice(graph_weight, (0, core * half), (depth, half))
    piece, _ = lax.optimization_barrier((piece, picked))
    pieces = [piece]
    for d in range(1, parts // 2):
        pieces.append(lax.ppermute(piece, "vert", [(i, (i + 2 * d) % parts) for i in range(parts)]))
    pieces = pieces + [swap_part(piece, 1) for piece in pieces]
    mine = jnp.stack(pieces)
    other = swap_core(mine)
    origin = [(part - 2 * d) % parts for d in range(parts // 2)]
    origin = jnp.stack(origin + [i ^ 1 for i in origin] + [core, 1 - core]).astype(jnp.int32)

    edges = block_values[0].reshape(own, -1)
    boundary = arrived.reshape(sources * most_rows, width)
    blocks = ROW_BLOCKS
    rows = own // blocks
    *chunks, mixed = call(
        mix_kernel,
        (*[shaped(rows, width)] * blocks, shaped(own, width)),
        (block_index[0], inputs, boundary, edges),
        flops=2 * edges.size * width,
        scratch=[pltpu.VMEM((own + sources * most_rows, width), jnp.bfloat16)],
    )
    chunks, fetched = lax.optimization_barrier((chunks, fetched))
    lower = [
        [
            lax.ppermute(chunk, "tm", [(i, i + CORES * d) for i in range(steps - CORES * d)])
            for d in range(1, chips)
        ]
        for chunk in chunks
    ]
    weight, hidden = call(
        assemble_kernel,
        (shaped(width, width), shaped(own, width)),
        (origin, mine, other, mixed),
        flops=2 * own * width * width,
    )
    sibling = swap_core(hidden)

    groups = [[head_weight]]
    spots = [step * shares + i for i in range(shares)]
    for d in range(1, chips):
        block = (step - CORES * d) % steps
        group = fetched[d - 1]
        if shared:
            middle = heads // 4
            groups.append([group, swap_part(group[:middle], 1), swap_part(group[middle:], 2)])
            spots += [block * 2 + share, block * 2 + 1 - share]
        else:
            groups.append([group])
            spots.append(block)
    place = jnp.stack(spots + [i ^ shares for i in spots]).astype(jnp.int32)
    owned = []
    for group in groups:
        size = heads * head_size
        piece = min(size, LANES)
        count = size // piece
        owned.append(call(
            functools.partial(own_kernel, len(group)),
            (
                shaped(count, 2 * piece, width),
                shaped(CORES, count, own, piece),
                shaped(CORES, count, own, 2 * piece),
            ),
            (hidden, sibling, *group),
            flops=2 * CORES * own * width * 3 * size,
            scratch=[
                pltpu.VMEM((count, piece, width), jnp.bfloat16),
                pltpu.VMEM((CORES * own, width), jnp.bfloat16),
            ],
        ))
    pairs, queries, boths = zip(*owned)

    slots = CORES * chips
    flags = [jnp.bool_(True), core == 1, core == 0, jnp.bool_(True)]
    reach = [chip >= d for d in range(1, chips) for _ in range(CORES)]
    flags = jnp.stack([*flags[:2], *reach, *flags[2:], *reach]).astype(jnp.int32)
    total = sum(a.shape[1] * a.shape[3] for a in queries)
    combined = []
    for r in range(blocks):
        mixed_rows = [a for chunk in lower[r] for a in (chunk, swap_core(chunk))]
        cut = lambda a: pl.BlockSpec((*a.shape[:2], rows, a.shape[3]), lambda _, r=r: (0, 0, r, 0))
        keep, send = call(
            functools.partial(attend_kernel, len(groups), head_size),
            (shaped(rows, total), shaped(rows, total)),
            (flags, weight, *pairs, *queries, *boths, *mixed_rows),
            specs=[SMEM, VMEM] + [VMEM] * len(pairs) + [cut(a) for a in (*queries, *boths)] + [VMEM] * len(mixed_rows),
            flops=2 * len(mixed_rows) * rows * width * (2 * total + width),
            scratch=[pltpu.VMEM((len(mixed_rows) * rows, width), jnp.bfloat16)],
        )
        line = pl.BlockSpec((rows, width), lambda _, r=r: (r, 0))
        combined = [call(
            functools.partial(combine_kernel, len(spots)),
            shaped(own, width),
            (place, hidden, keep, swap_core(send), *combined),
            specs=[SMEM, line, VMEM, VMEM] + [pl.BlockSpec(memory_space=pl.ANY)] * len(combined),
            out_specs=line,
            aliases={4: 0} if combined else None,
        )]
    return combined[0][None]


def solution(mesh):
    return jax.shard_map(
        functools.partial(shards, dict(mesh.shape)),
        mesh=mesh,
        in_specs=(
            P("tm", "vert", None),
            P("vert", None),
            P("tm", None, None),
            P("tm", "vert", None, None),
            P("tm", "vert", None),
            P("tm", "vert", None),
            P("tm", "vert", None, None),
        ),
        out_specs=P("tm", "vert", None),
        check_vma=False,
    )
```

```python
import functools
import math

import jax
import jax.numpy as jnp
from jax import lax
from jax.experimental import pallas as pl
from jax.experimental.pallas import tpu as pltpu
from jax.sharding import PartitionSpec as P

CORES = 2
ROW_CUTS = (0, 5, 8)
VMEM = pl.BlockSpec(memory_space=pltpu.VMEM)
SMEM = pl.BlockSpec(memory_space=pltpu.SMEM)
MASKED = -1e30
LANES = 128
PIECE = 256
NT = (((1,), (1,)), ((), ()))
TN = (((0,), (0,)), ((), ()))


def call(kernel, outs, ins, specs=None, out_specs=None, flops=0, scratch=(), limit=16, aliases=None, seconds=0):
    return pl.pallas_call(
        kernel,
        out_shape=outs,
        grid=(1,) if specs else (),
        in_specs=specs or [SMEM if a.dtype == jnp.int32 else VMEM for a in ins],
        out_specs=out_specs or jax.tree.map(lambda _: VMEM, outs),
        scratch_shapes=scratch,
        input_output_aliases=aliases or {},
        compiler_params=pltpu.CompilerParams(vmem_limit_bytes=limit * 2**20),
        cost_estimate=pl.CostEstimate(flops=int(seconds * 1e15), bytes_accessed=0, transcendentals=0),
    )(*ins)


def shaped(*shape, dtype=jnp.bfloat16):
    return jax.ShapeDtypeStruct(shape, dtype)


def after(value, token):
    return lax.optimization_barrier((value, token))[0]


def pick_kernel(row_ref, own_ref, picked_ref):
    shape = (own_ref.shape[0], row_ref.shape[1])
    chosen = (lax.broadcasted_iota(jnp.int32, shape, 0) == row_ref[...]).astype(jnp.bfloat16)
    picked_ref[...] = lax.dot_general(
        chosen, own_ref[...], TN, preferred_element_type=jnp.float32
    ).astype(picked_ref.dtype)


def mix_own_kernel(index_ref, own_ref, edge_ref, partial_ref, outer_ref, dense_ref):
    own = own_ref.shape[0]
    block_rows, chosen = index_ref.shape
    size = own // block_rows
    for b in range(block_rows):
        rows = slice(b * size, (b + 1) * size)
        blocks = [edge_ref[k, rows, :] for k in range(chosen)]
        for j in range(block_rows + outer_ref.shape[1] // size):
            dense = jnp.zeros_like(blocks[0])
            for k in range(chosen):
                dense = jnp.where(index_ref[b, k] == j, blocks[k], dense)
            if j < block_rows:
                dense_ref[rows, j * size : (j + 1) * size] = dense
            else:
                outer_ref[rows, (j - block_rows) * size : (j - block_rows + 1) * size] = dense
    partial_ref[...] = own_ref[...].astype(jnp.float32) + jnp.dot(
        dense_ref[...], own_ref[...], preferred_element_type=jnp.float32
    )


def mix_outer_kernel(partial_ref, outer_ref, arrived_ref, *refs):
    *chunk_refs, mixed_ref = refs
    total = partial_ref[...] + jnp.dot(
        outer_ref[...], arrived_ref[...], preferred_element_type=jnp.float32
    )
    mixed = total.astype(mixed_ref.dtype)
    mixed_ref[...] = mixed
    at = 0
    for chunk_ref in chunk_refs:
        chunk_ref[...] = mixed[at : at + chunk_ref.shape[0]]
        at += chunk_ref.shape[0]


def stack_kernel(*refs):
    for i, ref in enumerate(refs[:-1]):
        refs[-1][i] = ref[...]


def relu_dot(left, right):
    total = jnp.dot(left, right, preferred_element_type=jnp.float32)
    return jnp.maximum(total, 0.0).astype(jnp.bfloat16)


def assemble_kernel(base, meta_ref, *refs):
    *piece_refs, mine_ref, other_ref, weight_ref, hidden_ref, hidden_other_ref = refs
    _, depth, half = piece_refs[0].shape
    at = base
    for first, second in zip(piece_refs[::2], piece_refs[1::2]):
        for i in range(first.shape[0]):
            row = pl.ds(pl.multiple_of(meta_ref[at] * depth, depth), depth)
            for ref, core in ((first, meta_ref[0]), (second, 1 - meta_ref[0])):
                weight_ref[row, pl.ds(pl.multiple_of(core * half, half), half)] = ref[i]
            at += 1
    hidden_ref[...] = relu_dot(mine_ref[...], weight_ref[...])
    hidden_other_ref[...] = relu_dot(other_ref[...], weight_ref[...])


def arrange_kernel(*refs):
    *weight_refs, ask_ref, pair_ref = refs
    width = ask_ref.shape[1]
    head_size = weight_refs[0].shape[1] // 3
    i = 0
    for ref in weight_refs:
        for j in range(ref.shape[0]):
            piece, start = divmod(i * head_size, width)
            here = slice(start, start + head_size)
            ask_ref[piece, here, :] = ref[j, :head_size, :]
            pair_ref[piece, here, :] = ref[j, head_size : 2 * head_size, :]
            here = slice(width + start, width + start + head_size)
            pair_ref[piece, here, :] = ref[j, 2 * head_size :, :]
            i += 1


def own_kernel(meta_ref, mine_ref, other_ref, ask_ref, pair_ref, query_ref, both_ref, stacked_ref):
    rows = mine_ref.shape[0]
    core = meta_ref[0]
    stacked_ref[:rows, :] = mine_ref[...]
    stacked_ref[rows:, :] = other_ref[...]
    for p in range(ask_ref.shape[0]):
        for weight_ref, out_ref in ((ask_ref, query_ref), (pair_ref, both_ref)):
            packed = lax.dot_general(
                stacked_ref[...], weight_ref[p], NT, preferred_element_type=jnp.float32
            ).astype(jnp.bfloat16)
            out_ref[core, p] = packed[:rows]
            out_ref[1 - core, p] = packed[rows:]


def attend_kernel(groups, head_size, start, meta_ref, weight_ref, *refs):
    pair_refs, query_refs, both_refs = refs[:groups], refs[groups : 2 * groups], refs[2 * groups : 3 * groups]
    *mixed_refs, mine_ref, other_ref, stacked_ref, attended_ref = refs[3 * groups :]
    rows = mine_ref.shape[0]
    here = slice(start, start + rows)
    for s, ref in enumerate(mixed_refs):
        stacked_ref[s * rows : (s + 1) * rows, :] = ref[...]
    raised = relu_dot(stacked_ref[...], weight_ref[...])
    scale = head_size ** (-0.5)
    folded = math.frexp(scale)[0] == 0.5
    at = 0
    for pair_ref, query_ref, both_ref in zip(pair_refs, query_refs, both_refs):
        pieces, double, _ = pair_ref.shape
        width = double // 2
        group = lambda axis: lax.broadcasted_iota(jnp.int32, (width, width), axis) // head_size
        spread = jnp.where(group(0) == group(1), scale if folded else 1.0, 0.0).astype(jnp.bfloat16)
        for p in range(pieces):
            packed = lax.dot_general(raised, pair_ref[p], NT, preferred_element_type=jnp.float32)
            lower = [packed[s * rows : (s + 1) * rows] for s in range(len(mixed_refs))]
            keys = [a[:, :width].astype(jnp.bfloat16) for a in lower]
            values = [a[:, width:] for a in lower]
            keys += [both_ref[u, p, here, :width] for u in range(CORES)]
            values += [both_ref[u, p, here, width:].astype(jnp.float32) for u in range(CORES)]
            for t in range(CORES):
                slots = len(lower) + t + 1
                query = query_ref[t, p, here, :]
                products = jnp.concatenate([query * key for key in keys[:slots]], axis=0)
                scores = jnp.dot(products, spread, preferred_element_type=jnp.float32)
                if not folded:
                    scores *= scale
                parts = [scores[u * rows : (u + 1) * rows] for u in range(slots)]
                for u in range(len(lower)):
                    parts[u] = jnp.where(meta_ref[1 + u // CORES] > 0, parts[u], MASKED)
                top = functools.reduce(jnp.maximum, parts)
                parts = [jnp.exp(part - top) for part in parts]
                total = functools.reduce(jnp.add, [a * b for a, b in zip(parts, values)])
                total *= 1.0 / functools.reduce(jnp.add, parts)
                attended_ref[t, :, at : at + width] = total.astype(attended_ref.dtype)
            at += width
    mine_ref[...] = attended_ref[meta_ref[0]]
    other_ref[...] = attended_ref[1 - meta_ref[0]]


def combine_kernel(blocks, pieces, base, meta_ref, hidden_ref, *refs):
    out_ref = refs[-1]
    width = refs[0].shape[1] // pieces
    lanes = width % LANES == 0
    at = 0
    for r in range(blocks):
        here = slice(at, at + refs[r].shape[0])
        at = here.stop
        whole = None if lanes else hidden_ref[here, :].astype(jnp.float32)
        for half in range(CORES):
            for p in range(pieces):
                start = meta_ref[base + half * pieces + p] * width
                attended = refs[half * blocks + r][:, p * width : (p + 1) * width]
                if lanes:
                    column = pl.ds(pl.multiple_of(start, width), width)
                    total = hidden_ref[here, column].astype(jnp.float32) + attended.astype(jnp.float32)
                    out_ref[here, column] = total.astype(out_ref.dtype)
                else:
                    shape = (width, out_ref.shape[1])
                    spot = lax.broadcasted_iota(jnp.int32, shape, 0) + start
                    spot = (spot == lax.broadcasted_iota(jnp.int32, shape, 1)).astype(jnp.bfloat16)
                    whole += jnp.dot(attended, spot, preferred_element_type=jnp.float32)
        if not lanes:
            out_ref[here, :] = whole.astype(out_ref.dtype)


def shards(sizes, features, graph_weight, head_weight, send_rows, send_count, block_index, block_values):
    steps, parts = sizes["tm"], sizes["vert"]
    chips = steps // CORES
    step, part = lax.axis_index("tm"), lax.axis_index("vert")
    core, chip = step % CORES, step // CORES
    swap_core = lambda a: lax.ppermute(a, "tm", [(i, i ^ 1) for i in range(steps)])
    swap_part = lambda a, bit: lax.ppermute(a, "vert", [(i, i ^ bit) for i in range(parts)])
    turn = lambda a, axis, by, n: lax.ppermute(a, axis, [(i, (i + by) % n) for i in range(n)])
    heads, head_rows, _ = head_weight.shape
    shared = heads % 2 == 0 and parts % 4 == 0
    shares = 2 if shared else 1
    share = (part >> 1) % shares

    around = [(part - 2 * d) % parts for d in range(parts // 2)]
    spots = [step * shares + i for i in range(shares)]
    for d in range(1, chips):
        block = (step - CORES * d) % steps * shares
        spots += [block + share, block + 1 - share] if shared else [block]
    meta = [core, *[chip >= d for d in range(1, chips)], *around, *[i ^ 1 for i in around]]
    meta = jnp.stack([jnp.asarray(i, jnp.int32) for i in meta + spots + [i ^ shares for i in spots]])
    arrays = (features, graph_weight, head_weight, send_rows, send_count, block_index, block_values)
    (features, graph_weight, head_weight, send_rows, send_count, block_index, block_values), meta = (
        lax.optimization_barrier((arrays, meta))
    )
    inputs = features[0]
    own, width = inputs.shape

    head_size = head_rows // 3
    sent = lax.dynamic_slice_in_dim(head_weight, share * (heads // shares), heads // shares, 0)
    fetched = [turn(sent, "tm", CORES * d, steps) for d in range(1, chips)]

    size = heads * head_size
    unit = min(size, PIECE)
    count = size // unit
    arrange = lambda group: call(
        arrange_kernel, (shaped(count, unit, width), shaped(count, 2 * unit, width)), group
    )

    rows_list = send_rows[0, 0]
    sources, most_rows = rows_list.shape
    live = jnp.arange(most_rows)[None, :] < send_count[0, 0][:, None]
    slots = jnp.where(live, rows_list, -1).reshape(1, -1)
    picked = call(
        pick_kernel, shaped(sources * most_rows, width), (slots, inputs),
        specs=[VMEM, VMEM], flops=2 * own * width * sources * most_rows,
    )
    arrived = lax.all_to_all(
        picked.reshape(sources, most_rows, width), "vert", split_axis=0, concat_axis=0, tiled=True
    ).reshape(picked.shape)

    edges = block_values[0].transpose(1, 0, 2)
    outer_size = sources * most_rows
    partial, outer = call(
        mix_own_kernel,
        (shaped(own, width, dtype=jnp.float32), shaped(own, outer_size)),
        (block_index[0], inputs, edges),
        flops=2 * own * own * width,
        scratch=[pltpu.VMEM((own, own), jnp.bfloat16)],
    )

    depth = graph_weight.shape[0]
    half = width // CORES
    piece = lax.dynamic_slice(graph_weight, (0, core * half), (depth, half))
    around = [turn(piece, "vert", 2 * d, parts) for d in range(1, parts // 2)]
    around = call(stack_kernel, shaped(parts // 2, depth, half), (piece, *around), seconds=4e-6)
    arrived, around, fetched, partial, outer = lax.optimization_barrier((arrived, around, fetched, partial, outer))
    across = swap_part(around, 1)

    cuts = [own * cut // ROW_CUTS[-1] for cut in ROW_CUTS]
    blocks = len(cuts) - 1
    *chunks, mixed = call(
        mix_outer_kernel,
        (*[shaped(b - a, width) for a, b in zip(cuts, cuts[1:])], shaped(own, width)),
        (partial, outer, arrived),
        flops=2 * outer.size * width,
    )
    lower = [
        [
            turn(chunk, "tm", CORES * d, steps)
            for d in range(1, chips)
        ]
        for chunk in chunks
    ]
    arranged = arrange([after(head_weight, mixed)])
    across = after(across, arranged)
    groups = []
    for group in fetched:
        groups.append([group, swap_part(group, 2)] if shared else [group])
    weight, hidden, sibling = call(
        functools.partial(assemble_kernel, chips),
        (shaped(width, width), shaped(own, width), shaped(own, width)),
        (
            meta, around, swap_core(around), across, swap_core(across), mixed, swap_core(mixed),
        ),
        flops=4 * own * width * width,
    )

    owned, pairs = [], []
    hidden, sibling, lower[0], groups = lax.optimization_barrier((hidden, sibling, lower[0], groups))
    for g in range(chips):
        ask, pair = arranged if g == 0 else arrange(groups[g - 1])
        pairs.append(pair)
        owned.append(call(
            own_kernel,
            (shaped(CORES, count, own, unit), shaped(CORES, count, own, 2 * unit)),
            (meta, hidden, sibling, ask, pair),
            scratch=[pltpu.VMEM((CORES * own, width), jnp.bfloat16)],
        ))
    queries, boths = zip(*owned)

    total = sum(a.shape[1] * a.shape[3] for a in queries)
    kept, got = [], []
    token = owned[0]
    for r in range(blocks):
        rows = cuts[r + 1] - cuts[r]
        chunk = after(lower[r], token)
        mixed_rows = [a for b in chunk for a in (b, swap_core(b))]
        keep, send = token = call(
            functools.partial(attend_kernel, chips, head_size, cuts[r]),
            (shaped(rows, total), shaped(rows, total)),
            (meta, weight, *pairs, *queries, *boths, *mixed_rows),
            limit=11 + len(mixed_rows) * rows * width // 2**17,
            flops=2 * len(mixed_rows) * rows * width * (2 * total + width),
            scratch=[
                pltpu.VMEM((len(mixed_rows) * rows, width), jnp.bfloat16),
                pltpu.VMEM((CORES, rows, total), jnp.bfloat16),
            ],
        )
        kept.append(keep)
        got.append(swap_core(send))
    combined = call(
        functools.partial(combine_kernel, blocks, len(spots), meta.size - 2 * len(spots)),
        shaped(own, width),
        (meta, hidden, *kept, *got),
    )
    return combined[None]


def solution(mesh):
    return jax.shard_map(
        functools.partial(shards, dict(mesh.shape)),
        mesh=mesh,
        in_specs=(
            P("tm", "vert", None),
            P("vert", None),
            P("tm", None, None),
            P("tm", "vert", None, None),
            P("tm", "vert", None),
            P("tm", "vert", None),
            P("tm", "vert", None, None),
        ),
        out_specs=P("tm", "vert", None),
        check_vma=False,
    )
```

```python
import functools
import math

import jax
import jax.numpy as jnp
from jax import lax
from jax.experimental import pallas as pl
from jax.experimental.pallas import tpu as pltpu
from jax.sharding import PartitionSpec as P

CORES = 2
ROW_CUTS = (0, 6, 8)
VMEM = pl.BlockSpec(memory_space=pltpu.VMEM)
SMEM = pl.BlockSpec(memory_space=pltpu.SMEM)
ANY = pl.BlockSpec(memory_space=pl.ANY)
MASKED = -1e30
LANES = 128
PIECE = 256
NT = (((1,), (1,)), ((), ()))
TN = (((0,), (0,)), ((), ()))


def call(kernel, outs, ins, specs=None, out_specs=None, flops=0, scratch=(), limit=16, aliases=None, seconds=0, grid=None):
    return pl.pallas_call(
        kernel,
        out_shape=outs,
        grid=(1,) if specs and grid is None else (),
        in_specs=specs or [SMEM if a.dtype == jnp.int32 else VMEM for a in ins],
        out_specs=out_specs or jax.tree.map(lambda _: VMEM, outs),
        scratch_shapes=scratch,
        input_output_aliases=aliases or {},
        compiler_params=pltpu.CompilerParams(vmem_limit_bytes=limit * 2**20),
        cost_estimate=pl.CostEstimate(flops=int(seconds * 1e15), bytes_accessed=0, transcendentals=0),
    )(*ins)


def shaped(*shape, dtype=jnp.bfloat16):
    return jax.ShapeDtypeStruct(shape, dtype)


def after(value, token):
    return lax.optimization_barrier((value, token))[0]


def pick_kernel(row_ref, own_ref, picked_ref):
    shape = (own_ref.shape[0], row_ref.shape[1])
    chosen = (lax.broadcasted_iota(jnp.int32, shape, 0) == row_ref[...]).astype(jnp.bfloat16)
    picked_ref[...] = lax.dot_general(
        chosen, own_ref[...], TN, preferred_element_type=jnp.float32
    ).astype(picked_ref.dtype)


def mix_kernel(index_ref, own_ref, edge_ref, arrived_ref, *refs):
    *chunk_refs, mixed_ref, dense_ref, outer_ref = refs
    own = own_ref.shape[0]
    block_rows, chosen = index_ref.shape
    size = own // block_rows
    for b in range(block_rows):
        rows = slice(b * size, (b + 1) * size)
        blocks = [edge_ref[k, rows, :] for k in range(chosen)]
        for j in range(block_rows + outer_ref.shape[1] // size):
            dense = jnp.zeros_like(blocks[0])
            for k in range(chosen):
                dense = jnp.where(index_ref[b, k] == j, blocks[k], dense)
            if j < block_rows:
                dense_ref[rows, j * size : (j + 1) * size] = dense
            else:
                outer_ref[rows, (j - block_rows) * size : (j - block_rows + 1) * size] = dense
    total = own_ref[...].astype(jnp.float32)
    total += jnp.dot(dense_ref[...], own_ref[...], preferred_element_type=jnp.float32)
    total += jnp.dot(outer_ref[...], arrived_ref[...], preferred_element_type=jnp.float32)
    mixed = total.astype(mixed_ref.dtype)
    mixed_ref[...] = mixed
    at = 0
    for chunk_ref in chunk_refs:
        chunk_ref[...] = mixed[at : at + chunk_ref.shape[0]]
        at += chunk_ref.shape[0]


def stack_kernel(*refs):
    *piece_refs, out_ref, sems = refs
    copies = [pltpu.make_async_copy(ref, out_ref.at[i], sems.at[i]) for i, ref in enumerate(piece_refs)]
    for copy in copies:
        copy.start()
    for copy in copies:
        copy.wait()


def relu_dot(left, right):
    total = jnp.dot(left, right, preferred_element_type=jnp.float32)
    return jnp.maximum(total, 0.0).astype(jnp.bfloat16)


def assemble_kernel(base, meta_ref, *refs):
    *piece_refs, mine_ref, other_ref, weight_ref, hidden_ref, hidden_other_ref = refs
    _, depth, half = piece_refs[0].shape
    at = base
    for first, second in zip(piece_refs[::2], piece_refs[1::2]):
        for i in range(first.shape[0]):
            row = pl.ds(pl.multiple_of(meta_ref[at] * depth, depth), depth)
            for ref, core in ((first, meta_ref[0]), (second, 1 - meta_ref[0])):
                weight_ref[row, pl.ds(pl.multiple_of(core * half, half), half)] = ref[i]
            at += 1
    hidden_ref[...] = relu_dot(mine_ref[...], weight_ref[...])
    hidden_other_ref[...] = relu_dot(other_ref[...], weight_ref[...])


def arrange_kernel(*refs):
    *weight_refs, ask_ref, pair_ref = refs
    width = ask_ref.shape[1]
    head_size = weight_refs[0].shape[1] // 3
    i = 0
    for ref in weight_refs:
        for j in range(ref.shape[0]):
            piece, start = divmod(i * head_size, width)
            here = slice(start, start + head_size)
            ask_ref[piece, here, :] = ref[j, :head_size, :]
            pair_ref[piece, here, :] = ref[j, head_size : 2 * head_size, :]
            here = slice(width + start, width + start + head_size)
            pair_ref[piece, here, :] = ref[j, 2 * head_size :, :]
            i += 1


def own_kernel(meta_ref, mine_ref, other_ref, ask_ref, pair_ref, query_ref, both_ref, stacked_ref):
    rows = mine_ref.shape[0]
    core = meta_ref[0]
    stacked_ref[:rows, :] = mine_ref[...]
    stacked_ref[rows:, :] = other_ref[...]
    for p in range(ask_ref.shape[0]):
        for weight_ref, out_ref in ((ask_ref, query_ref), (pair_ref, both_ref)):
            packed = lax.dot_general(
                stacked_ref[...], weight_ref[p], NT, preferred_element_type=jnp.float32
            ).astype(jnp.bfloat16)
            out_ref[core, p] = packed[:rows]
            out_ref[1 - core, p] = packed[rows:]


def attend_kernel(groups, head_size, start, meta_ref, weight_ref, *refs):
    pair_refs, query_refs, both_refs = refs[:groups], refs[groups : 2 * groups], refs[2 * groups : 3 * groups]
    *mixed_refs, mine_ref, other_ref, stacked_ref, attended_ref = refs[3 * groups :]
    rows = mine_ref.shape[0]
    here = slice(start, start + rows)
    for s, ref in enumerate(mixed_refs):
        stacked_ref[s * rows : (s + 1) * rows, :] = ref[...]
    raised = relu_dot(stacked_ref[...], weight_ref[...])
    scale = head_size ** (-0.5)
    folded = math.frexp(scale)[0] == 0.5
    at = 0
    for pair_ref, query_ref, both_ref in zip(pair_refs, query_refs, both_refs):
        pieces, double, _ = pair_ref.shape
        width = double // 2
        group = lambda axis: lax.broadcasted_iota(jnp.int32, (width, width), axis) // head_size
        spread = jnp.where(group(0) == group(1), scale if folded else 1.0, 0.0).astype(jnp.bfloat16)
        for p in range(pieces):
            packed = lax.dot_general(raised, pair_ref[p], NT, preferred_element_type=jnp.float32)
            lower = [packed[s * rows : (s + 1) * rows] for s in range(len(mixed_refs))]
            keys = [a[:, :width].astype(jnp.bfloat16) for a in lower]
            values = [a[:, width:] for a in lower]
            keys += [both_ref[u, p, here, :width] for u in range(CORES)]
            values += [both_ref[u, p, here, width:].astype(jnp.float32) for u in range(CORES)]
            for t in range(CORES):
                slots = len(lower) + t + 1
                query = query_ref[t, p, here, :]
                products = jnp.concatenate([query * key for key in keys[:slots]], axis=0)
                scores = jnp.dot(products, spread, preferred_element_type=jnp.float32)
                if not folded:
                    scores *= scale
                parts = [scores[u * rows : (u + 1) * rows] for u in range(slots)]
                for u in range(len(lower)):
                    parts[u] = jnp.where(meta_ref[1 + u // CORES] > 0, parts[u], MASKED)
                top = functools.reduce(jnp.maximum, parts)
                parts = [jnp.exp(part - top) for part in parts]
                total = functools.reduce(jnp.add, [a * b for a, b in zip(parts, values)])
                total *= 1.0 / functools.reduce(jnp.add, parts)
                attended_ref[t, :, at : at + width] = total.astype(attended_ref.dtype)
            at += width
    mine_ref[...] = attended_ref[meta_ref[0]]
    other_ref[...] = attended_ref[1 - meta_ref[0]]


def combine_kernel(blocks, pieces, base, meta_ref, hidden_ref, *refs):
    out_ref = refs[-1]
    width = refs[0].shape[1] // pieces
    lanes = width % LANES == 0
    at = 0
    for r in range(blocks):
        here = slice(at, at + refs[r].shape[0])
        at = here.stop
        whole = None if lanes else hidden_ref[here, :].astype(jnp.float32)
        for half in range(CORES):
            for p in range(pieces):
                start = meta_ref[base + half * pieces + p] * width
                attended = refs[half * blocks + r][:, p * width : (p + 1) * width]
                if lanes:
                    column = pl.ds(pl.multiple_of(start, width), width)
                    total = hidden_ref[here, column].astype(jnp.float32) + attended.astype(jnp.float32)
                    out_ref[here, column] = total.astype(out_ref.dtype)
                else:
                    shape = (width, out_ref.shape[1])
                    spot = lax.broadcasted_iota(jnp.int32, shape, 0) + start
                    spot = (spot == lax.broadcasted_iota(jnp.int32, shape, 1)).astype(jnp.bfloat16)
                    whole += jnp.dot(attended, spot, preferred_element_type=jnp.float32)
        if not lanes:
            out_ref[here, :] = whole.astype(out_ref.dtype)


def shards(sizes, features, graph_weight, head_weight, send_rows, send_count, block_index, block_values):
    steps, parts = sizes["tm"], sizes["vert"]
    chips = steps // CORES
    step, part = lax.axis_index("tm"), lax.axis_index("vert")
    core, chip = step % CORES, step // CORES
    swap_core = lambda a: lax.ppermute(a, "tm", [(i, i ^ 1) for i in range(steps)])
    swap_part = lambda a, bit: lax.ppermute(a, "vert", [(i, i ^ bit) for i in range(parts)])
    turn = lambda a, axis, by, n: lax.ppermute(a, axis, [(i, (i + by) % n) for i in range(n)])
    heads, head_rows, _ = head_weight.shape
    shared = heads % 2 == 0 and parts % 4 == 0
    shares = 2 if shared else 1
    share = (part >> 1) % shares

    around = [(part - 2 * d) % parts for d in range(parts // 2)]
    spots = [step * shares + i for i in range(shares)]
    for d in range(1, chips):
        block = (step - CORES * d) % steps * shares
        spots += [block + share, block + 1 - share] if shared else [block]
    meta = [core, *[chip >= d for d in range(1, chips)], *around, *[i ^ 1 for i in around]]
    meta = jnp.stack([jnp.asarray(i, jnp.int32) for i in meta + spots + [i ^ shares for i in spots]])
    arrays = (features, graph_weight, head_weight, send_rows, send_count, block_index, block_values)
    (features, graph_weight, head_weight, send_rows, send_count, block_index, block_values), meta = (
        lax.optimization_barrier((arrays, meta))
    )
    inputs = features[0]
    own, width = inputs.shape

    head_size = head_rows // 3
    sent = lax.dynamic_slice_in_dim(head_weight, share * (heads // shares), heads // shares, 0)
    fetched = [turn(sent, "tm", CORES * d, steps) for d in range(1, chips)]

    size = heads * head_size
    unit = min(size, PIECE)
    count = size // unit
    arrange = lambda group, seconds=0: call(
        arrange_kernel, (shaped(count, unit, width), shaped(count, 2 * unit, width)), group, seconds=seconds
    )

    rows_list = send_rows[0, 0]
    sources, most_rows = rows_list.shape
    live = jnp.arange(most_rows)[None, :] < send_count[0, 0][:, None]
    slots = jnp.where(live, rows_list, -1).reshape(1, -1)
    picked = call(
        pick_kernel, shaped(sources * most_rows, width), (slots, inputs),
        specs=[VMEM, VMEM], flops=2 * own * width * sources * most_rows,
    )
    arrived = lax.all_to_all(
        picked.reshape(sources, most_rows, width), "vert", split_axis=0, concat_axis=0, tiled=True
    ).reshape(picked.shape)

    depth = graph_weight.shape[0]
    half = width // CORES
    piece = lax.dynamic_slice(graph_weight, (0, core * half), (depth, half))
    around = [turn(piece, "vert", 2 * d, parts) for d in range(1, parts // 2)]
    around = call(
        stack_kernel, shaped(parts // 2, depth, half), (piece, *around),
        specs=[ANY] * (parts // 2), grid=(), limit=16, seconds=4e-6,
        scratch=[pltpu.SemaphoreType.DMA((parts // 2,))],
    )
    across = swap_part(around, 1)

    cuts = [own * cut // ROW_CUTS[-1] for cut in ROW_CUTS]
    blocks = len(cuts) - 1
    outer_size = sources * most_rows
    *chunks, mixed = call(
        mix_kernel,
        (*[shaped(b - a, width) for a, b in zip(cuts, cuts[1:])], shaped(own, width)),
        (block_index[0], inputs, block_values[0].transpose(1, 0, 2), arrived),
        scratch=[pltpu.VMEM((own, own), jnp.bfloat16), pltpu.VMEM((own, outer_size), jnp.bfloat16)],
    )
    lower = [
        [
            turn(chunk, "tm", CORES * d, steps)
            for d in range(1, chips)
        ]
        for chunk in chunks
    ]
    arranged = arrange([after(head_weight, mixed)])
    across = after(across, arranged)
    groups = []
    for group in fetched:
        groups.append([group, swap_part(group, 2)] if shared else [group])
    weight, hidden, sibling = call(
        functools.partial(assemble_kernel, chips),
        (shaped(width, width), shaped(own, width), shaped(own, width)),
        (
            meta, around, swap_core(around), across, swap_core(across), mixed, swap_core(mixed),
        ),
        flops=4 * own * width * width,
    )

    owned, pairs = [], []
    for g in range(chips):
        if g == 1:
            owned, lower[0], groups = lax.optimization_barrier((owned, lower[0], groups))
        ask, pair = arranged if g == 0 else arrange(groups[g - 1], 12e-6)
        pairs.append(pair)
        owned.append(call(
            own_kernel,
            (shaped(CORES, count, own, unit), shaped(CORES, count, own, 2 * unit)),
            (meta, hidden, sibling, ask, pair),
            scratch=[pltpu.VMEM((CORES * own, width), jnp.bfloat16)],
        ))
    queries, boths = zip(*owned)

    total = sum(a.shape[1] * a.shape[3] for a in queries)
    kept, got = [], []
    token = owned[0]
    for r in range(blocks):
        rows = cuts[r + 1] - cuts[r]
        chunk = after(lower[r], token)
        mixed_rows = [a for b in chunk for a in (b, swap_core(b))]
        keep, send = token = call(
            functools.partial(attend_kernel, chips, head_size, cuts[r]),
            (shaped(rows, total), shaped(rows, total)),
            (meta, weight, *pairs, *queries, *boths, *mixed_rows),
            limit=11 + len(mixed_rows) * rows * width // 2**17,
            flops=2 * len(mixed_rows) * rows * width * (2 * total + width),
            scratch=[
                pltpu.VMEM((len(mixed_rows) * rows, width), jnp.bfloat16),
                pltpu.VMEM((CORES, rows, total), jnp.bfloat16),
            ],
        )
        kept.append(keep)
        got.append(swap_core(send))
    combined = call(
        functools.partial(combine_kernel, blocks, len(spots), meta.size - 2 * len(spots)),
        shaped(own, width),
        (meta, hidden, *kept, *got),
    )
    return combined[None]


def solution(mesh):
    return jax.shard_map(
        functools.partial(shards, dict(mesh.shape)),
        mesh=mesh,
        in_specs=(
            P("tm", "vert", None),
            P("vert", None),
            P("tm", None, None),
            P("tm", "vert", None, None),
            P("tm", "vert", None),
            P("tm", "vert", None),
            P("tm", "vert", None, None),
        ),
        out_specs=P("tm", "vert", None),
        check_vma=False,
    )
```

```python
import functools
import math

import jax
import jax.numpy as jnp
from jax import lax
from jax.experimental import pallas as pl
from jax.experimental.pallas import tpu as pltpu
from jax.sharding import PartitionSpec as P

CORES = 2
ROW_CUTS = (0, 6, 8)
VMEM = pl.BlockSpec(memory_space=pltpu.VMEM)
SMEM = pl.BlockSpec(memory_space=pltpu.SMEM)
ANY = pl.BlockSpec(memory_space=pl.ANY)
MASKED = -1e30
LANES = 128
PIECE = 256
NT = (((1,), (1,)), ((), ()))
TN = (((0,), (0,)), ((), ()))


def call(kernel, outs, ins, specs=None, out_specs=None, flops=0, scratch=(), limit=16, aliases=None, seconds=0, grid=None):
    return pl.pallas_call(
        kernel,
        out_shape=outs,
        grid=(1,) if specs and grid is None else (),
        in_specs=specs or [SMEM if a.dtype == jnp.int32 else VMEM for a in ins],
        out_specs=out_specs or jax.tree.map(lambda _: VMEM, outs),
        scratch_shapes=scratch,
        input_output_aliases=aliases or {},
        compiler_params=pltpu.CompilerParams(vmem_limit_bytes=limit * 2**20),
        cost_estimate=pl.CostEstimate(flops=int(seconds * 1e15), bytes_accessed=0, transcendentals=0),
    )(*ins)


def shaped(*shape, dtype=jnp.bfloat16):
    return jax.ShapeDtypeStruct(shape, dtype)


def after(value, token):
    return lax.optimization_barrier((value, token))[0]


def pick_kernel(row_ref, own_ref, picked_ref):
    shape = (own_ref.shape[0], row_ref.shape[1])
    chosen = (lax.broadcasted_iota(jnp.int32, shape, 0) == row_ref[...]).astype(jnp.bfloat16)
    picked_ref[...] = lax.dot_general(
        chosen, own_ref[...], TN, preferred_element_type=jnp.float32
    ).astype(picked_ref.dtype)


def mix_kernel(index_ref, own_ref, edge_ref, arrived_ref, *refs):
    *chunk_refs, mixed_ref, dense_ref, outer_ref = refs
    own = own_ref.shape[0]
    block_rows, chosen = index_ref.shape
    size = own // block_rows
    for b in range(block_rows):
        rows = slice(b * size, (b + 1) * size)
        blocks = [edge_ref[k, rows, :] for k in range(chosen)]
        for j in range(block_rows + outer_ref.shape[1] // size):
            dense = jnp.zeros_like(blocks[0])
            for k in range(chosen):
                dense = jnp.where(index_ref[b, k] == j, blocks[k], dense)
            if j < block_rows:
                dense_ref[rows, j * size : (j + 1) * size] = dense
            else:
                outer_ref[rows, (j - block_rows) * size : (j - block_rows + 1) * size] = dense
    total = own_ref[...].astype(jnp.float32)
    total += jnp.dot(dense_ref[...], own_ref[...], preferred_element_type=jnp.float32)
    total += jnp.dot(outer_ref[...], arrived_ref[...], preferred_element_type=jnp.float32)
    mixed = total.astype(mixed_ref.dtype)
    mixed_ref[...] = mixed
    at = 0
    for chunk_ref in chunk_refs:
        chunk_ref[...] = mixed[at : at + chunk_ref.shape[0]]
        at += chunk_ref.shape[0]


def stack_kernel(*refs):
    *piece_refs, out_ref, sems = refs
    copies = [pltpu.make_async_copy(ref, out_ref.at[i], sems.at[i]) for i, ref in enumerate(piece_refs)]
    for copy in copies:
        copy.start()
    for copy in copies:
        copy.wait()


def relu_dot(left, right):
    total = jnp.dot(left, right, preferred_element_type=jnp.float32)
    return jnp.maximum(total, 0.0).astype(jnp.bfloat16)


def assemble_kernel(base, meta_ref, *refs):
    *piece_refs, mine_ref, other_ref, weight_ref, hidden_ref, hidden_other_ref = refs
    _, depth, half = piece_refs[0].shape
    at = base
    for first, second in zip(piece_refs[::2], piece_refs[1::2]):
        for i in range(first.shape[0]):
            row = pl.ds(pl.multiple_of(meta_ref[at] * depth, depth), depth)
            for ref, core in ((first, meta_ref[0]), (second, 1 - meta_ref[0])):
                weight_ref[row, pl.ds(pl.multiple_of(core * half, half), half)] = ref[i]
            at += 1
    hidden_ref[...] = relu_dot(mine_ref[...], weight_ref[...])
    hidden_other_ref[...] = relu_dot(other_ref[...], weight_ref[...])


def arrange_kernel(heads_ref, rows_ref):
    heads, head_rows, _ = heads_ref.shape
    size = head_rows // 3
    for h in range(heads):
        for i in range(3):
            start = (i * heads + h) * size
            rows_ref[start : start + size, :] = heads_ref[h, i * size : (i + 1) * size, :]


def own_kernel(meta_ref, mine_ref, other_ref, rows_ref, query_ref, both_ref, stacked_ref):
    rows = mine_ref.shape[0]
    width = query_ref.shape[2]
    core = meta_ref[0]
    stacked_ref[:rows, :] = mine_ref[...]
    stacked_ref[rows:, :] = other_ref[...]
    packed = lax.dot_general(
        stacked_ref[...], rows_ref[...], NT, preferred_element_type=jnp.float32
    ).astype(jnp.bfloat16)
    for t, slot in enumerate((core, 1 - core)):
        part = packed[t * rows : (t + 1) * rows]
        query_ref[slot] = part[:, :width]
        both_ref[slot] = part[:, width:]


def arrange_own_kernel(meta_ref, mine_ref, other_ref, heads_ref, rows_ref, query_ref, both_ref, stacked_ref):
    arrange_kernel(heads_ref, rows_ref)
    own_kernel(meta_ref, mine_ref, other_ref, rows_ref, query_ref, both_ref, stacked_ref)


def attend_kernel(lists, head_size, start, meta_ref, weight_ref, *refs):
    total = sum(lists)
    rows_refs, query_refs, both_refs = refs[:total], refs[total : 2 * total], refs[2 * total : 3 * total]
    *mixed_refs, mine_ref, other_ref, stacked_ref, attended_ref = refs[3 * total :]
    rows = mine_ref.shape[0]
    here = slice(start, start + rows)
    slot = lambda s: slice(s * rows, (s + 1) * rows)
    for s, ref in enumerate(mixed_refs):
        stacked_ref[slot(s), :] = ref[...]
    raised = relu_dot(stacked_ref[...], weight_ref[...])
    scale = head_size ** (-0.5)
    folded = math.frexp(scale)[0] == 0.5
    at = 0
    for g, count in enumerate(lists):
        members = range(sum(lists[:g]), sum(lists[: g + 1]))
        packed = []
        for m in members:
            first = query_refs[m].shape[2]
            packed.append(lax.dot_general(
                raised, rows_refs[m][first:, :], NT, preferred_element_type=jnp.float32
            ))
        join = lambda parts: jnp.concatenate(parts, axis=1) if len(parts) > 1 else parts[0]
        half = packed[0].shape[1] // 2
        key = join([a[:, :half] for a in packed]).astype(jnp.bfloat16)
        value = join([a[:, half:] for a in packed])
        keys = [key[slot(s)] for s in range(len(mixed_refs))]
        values = [value[slot(s)] for s in range(len(mixed_refs))]
        keys += [join([both_refs[m][u, here, :half] for m in members]) for u in range(CORES)]
        values += [
            join([both_refs[m][u, here, half:] for m in members]).astype(jnp.float32) for u in range(CORES)
        ]
        size = key.shape[1]
        group = lambda axis: lax.broadcasted_iota(jnp.int32, (size, size), axis) // head_size
        spread = jnp.where(group(0) == group(1), scale if folded else 1.0, 0.0).astype(jnp.bfloat16)
        for t in range(CORES):
            slots = len(mixed_refs) + t + 1
            query = join([query_refs[m][t, here, :] for m in members])
            products = jnp.concatenate([query * k for k in keys[:slots]], axis=0)
            scores = jnp.dot(products, spread, preferred_element_type=jnp.float32)
            if not folded:
                scores *= scale
            parts = [scores[slot(u)] for u in range(slots)]
            for u in range(len(mixed_refs)):
                parts[u] = jnp.where(meta_ref[1 + u // CORES] > 0, parts[u], MASKED)
            top = functools.reduce(jnp.maximum, parts)
            parts = [jnp.exp(part - top) for part in parts]
            result = functools.reduce(jnp.add, [a * b for a, b in zip(parts, values)])
            result *= 1.0 / functools.reduce(jnp.add, parts)
            attended_ref[t, :, at : at + size] = result.astype(attended_ref.dtype)
        at += size
    mine_ref[...] = attended_ref[meta_ref[0]]
    other_ref[...] = attended_ref[1 - meta_ref[0]]


def combine_kernel(blocks, pieces, base, meta_ref, hidden_ref, *refs):
    *refs, out_ref, sum_ref, sems = refs
    width = refs[0].shape[1] // pieces
    lanes = width % LANES == 0
    step = math.gcd(*[ref.shape[0] for ref in refs])
    copies = []
    at = 0
    for r in range(blocks):
        for first in range(0, refs[r].shape[0], step):
            rows = slice(first, first + step)
            here = slice(at, at + step)
            whole = None if lanes else hidden_ref[here, :].astype(jnp.float32)
            for half in range(CORES):
                for p in range(pieces):
                    start = meta_ref[base + half * pieces + p] * width
                    attended = refs[half * blocks + r][rows, p * width : (p + 1) * width]
                    if lanes:
                        column = pl.ds(pl.multiple_of(start, width), width)
                        total = hidden_ref[here, column].astype(jnp.float32) + attended.astype(jnp.float32)
                        sum_ref[here, column] = total.astype(sum_ref.dtype)
                    else:
                        shape = (width, out_ref.shape[1])
                        spot = lax.broadcasted_iota(jnp.int32, shape, 0) + start
                        spot = (spot == lax.broadcasted_iota(jnp.int32, shape, 1)).astype(jnp.bfloat16)
                        whole += jnp.dot(attended, spot, preferred_element_type=jnp.float32)
            if not lanes:
                sum_ref[here, :] = whole.astype(sum_ref.dtype)
            copies.append(pltpu.make_async_copy(sum_ref.at[here], out_ref.at[here], sems.at[len(copies)]))
            copies[-1].start()
            at += step
    for copy in copies:
        copy.wait()


def shards(sizes, features, graph_weight, head_weight, send_rows, send_count, block_index, block_values):
    steps, parts = sizes["tm"], sizes["vert"]
    chips = steps // CORES
    step, part = lax.axis_index("tm"), lax.axis_index("vert")
    core, chip = step % CORES, step // CORES
    swap_core = lambda a: lax.ppermute(a, "tm", [(i, i ^ 1) for i in range(steps)])
    swap_part = lambda a, bit: lax.ppermute(a, "vert", [(i, i ^ bit) for i in range(parts)])
    turn = lambda a, axis, by, n: lax.ppermute(a, axis, [(i, (i + by) % n) for i in range(n)])
    heads, head_rows, _ = head_weight.shape
    shared = heads % 2 == 0 and parts % 4 == 0
    shares = 2 if shared else 1
    share = (part >> 1) % shares

    around = [(part - 2 * d) % parts for d in range(parts // 2)]
    spots = [step * shares + i for i in range(shares)]
    for d in range(1, chips):
        block = (step - CORES * d) % steps * shares
        spots += [block + share, block + 1 - share] if shared else [block]
    meta = [core, *[chip >= d for d in range(1, chips)], *around, *[i ^ 1 for i in around]]
    meta = jnp.stack([jnp.asarray(i, jnp.int32) for i in meta + spots + [i ^ shares for i in spots]])
    arrays = (features, graph_weight, head_weight, send_rows, send_count, block_index, block_values)
    (features, graph_weight, head_weight, send_rows, send_count, block_index, block_values), meta = (
        lax.optimization_barrier((arrays, meta))
    )
    inputs = features[0]
    own, width = inputs.shape

    head_size = head_rows // 3
    sent = lax.dynamic_slice_in_dim(head_weight, share * (heads // shares), heads // shares, 0)
    fetched = [turn(sent, "tm", CORES * d, steps) for d in range(1, chips)]

    rows_list = send_rows[0, 0]
    sources, most_rows = rows_list.shape
    live = jnp.arange(most_rows)[None, :] < send_count[0, 0][:, None]
    slots = jnp.where(live, rows_list, -1).reshape(1, -1)
    picked = call(
        pick_kernel, shaped(sources * most_rows, width), (slots, inputs),
        specs=[VMEM, VMEM], flops=2 * own * width * sources * most_rows,
    )
    arrived = lax.all_to_all(
        picked.reshape(sources, most_rows, width), "vert", split_axis=0, concat_axis=0, tiled=True
    ).reshape(picked.shape)

    depth = graph_weight.shape[0]
    half = width // CORES
    piece = lax.dynamic_slice(graph_weight, (0, core * half), (depth, half))
    around = [turn(piece, "vert", 2 * d, parts) for d in range(1, parts // 2)]
    around = call(
        stack_kernel, shaped(parts // 2, depth, half), (piece, *around),
        specs=[ANY] * (parts // 2), grid=(), limit=16, seconds=4e-6,
        scratch=[pltpu.SemaphoreType.DMA((parts // 2,))],
    )
    across = swap_part(around, 1)

    cuts = [own * cut // ROW_CUTS[-1] for cut in ROW_CUTS]
    blocks = len(cuts) - 1
    outer_size = sources * most_rows
    *chunks, mixed = call(
        mix_kernel,
        (*[shaped(b - a, width) for a, b in zip(cuts, cuts[1:])], shaped(own, width)),
        (block_index[0], inputs, block_values[0].transpose(1, 0, 2), arrived),
        scratch=[pltpu.VMEM((own, own), jnp.bfloat16), pltpu.VMEM((own, outer_size), jnp.bfloat16)],
    )
    lower = [
        [
            turn(chunk, "tm", CORES * d, steps)
            for d in range(1, chips)
        ]
        for chunk in chunks
    ]
    arranged = call(arrange_kernel, shaped(heads * head_rows, width), (after(head_weight, mixed),))
    across = after(across, arranged)
    groups = [[group, swap_part(group, 2)] if shared else [group] for group in fetched]
    weight, hidden, sibling = call(
        functools.partial(assemble_kernel, chips),
        (shaped(width, width), shaped(own, width), shaped(own, width)),
        (
            meta, around, swap_core(around), across, swap_core(across), mixed, swap_core(mixed),
        ),
        flops=4 * own * width * width,
    )

    def place(weights, ready=None, seconds=0):
        count = weights.shape[0] // 3 if ready else weights.shape[0] * head_size
        outs = (shaped(CORES, own, count), shaped(CORES, own, 2 * count))
        if not ready:
            outs = (shaped(3 * count, width), *outs)
        result = call(
            own_kernel if ready else arrange_own_kernel,
            outs,
            (meta, hidden, sibling, weights),
            seconds=seconds,
            scratch=[pltpu.VMEM((CORES * own, width), jnp.bfloat16)],
        )
        return (weights, *result) if ready else result

    owned = [place(arranged, True)]
    for group in groups:
        group = list(group)
        for i, weights in enumerate(group):
            if i == len(group) - 1:
                owned, lower[0], weights = lax.optimization_barrier((owned, lower[0], weights))
            owned.append(place(weights, seconds=12e-6 if i == len(group) - 1 else 0))
    lists = [1, *[len(group) for group in groups]]

    total = chips * heads * head_size
    kept, got = [], []
    token = owned[0][1]
    for r in range(blocks):
        rows = cuts[r + 1] - cuts[r]
        chunk = after(lower[r], token)
        mixed_rows = [a for b in chunk for a in (b, swap_core(b))]
        keep, send = token = call(
            functools.partial(attend_kernel, lists, head_size, cuts[r]),
            (shaped(rows, total), shaped(rows, total)),
            (meta, weight, *[a[i] for i in range(3) for a in owned], *mixed_rows),
            limit=11 + len(mixed_rows) * rows * width // 2**17,
            flops=2 * len(mixed_rows) * rows * width * (2 * total + width),
            scratch=[
                pltpu.VMEM((len(mixed_rows) * rows, width), jnp.bfloat16),
                pltpu.VMEM((CORES, rows, total), jnp.bfloat16),
            ],
        )
        kept.append(keep)
        got.append(swap_core(send))
    combined = call(
        functools.partial(combine_kernel, blocks, len(spots), meta.size - 2 * len(spots)),
        shaped(own, width),
        (meta, hidden, *kept, *got),
        out_specs=ANY,
        scratch=[
            pltpu.VMEM((own, width), jnp.bfloat16),
            pltpu.SemaphoreType.DMA((own // math.gcd(*[a.shape[0] for a in kept]),)),
        ],
    )
    return combined[None]


def solution(mesh):
    return jax.shard_map(
        functools.partial(shards, dict(mesh.shape)),
        mesh=mesh,
        in_specs=(
            P("tm", "vert", None),
            P("vert", None),
            P("tm", None, None),
            P("tm", "vert", None, None),
            P("tm", "vert", None),
            P("tm", "vert", None),
            P("tm", "vert", None, None),
        ),
        out_specs=P("tm", "vert", None),
        check_vma=False,
    )
```

```python
import functools
import math

import jax
import jax.numpy as jnp
from jax import lax
from jax.experimental import pallas as pl
from jax.experimental.pallas import tpu as pltpu
from jax.sharding import PartitionSpec as P

CORES = 2
ROW_CUTS = (0, 6, 8)
VMEM = pl.BlockSpec(memory_space=pltpu.VMEM)
SMEM = pl.BlockSpec(memory_space=pltpu.SMEM)
ANY = pl.BlockSpec(memory_space=pl.ANY)
MASKED = -1e30
LANES = 128
PIECE = 256
NT = (((1,), (1,)), ((), ()))
TN = (((0,), (0,)), ((), ()))


def call(kernel, outs, ins, specs=None, out_specs=None, flops=0, scratch=(), limit=16, aliases=None, seconds=0, grid=None):
    return pl.pallas_call(
        kernel,
        out_shape=outs,
        grid=(1,) if specs and grid is None else (),
        in_specs=specs or [SMEM if a.dtype == jnp.int32 else VMEM for a in ins],
        out_specs=out_specs or jax.tree.map(lambda _: VMEM, outs),
        scratch_shapes=scratch,
        input_output_aliases=aliases or {},
        compiler_params=pltpu.CompilerParams(vmem_limit_bytes=limit * 2**20),
        cost_estimate=pl.CostEstimate(flops=int(seconds * 1e15), bytes_accessed=0, transcendentals=0),
    )(*ins)


def shaped(*shape, dtype=jnp.bfloat16):
    return jax.ShapeDtypeStruct(shape, dtype)


def after(value, token):
    return lax.optimization_barrier((value, token))[0]


def pick_kernel(row_ref, own_ref, picked_ref):
    shape = (own_ref.shape[0], row_ref.shape[1])
    chosen = (lax.broadcasted_iota(jnp.int32, shape, 0) == row_ref[...]).astype(jnp.bfloat16)
    picked_ref[...] = lax.dot_general(
        chosen, own_ref[...], TN, preferred_element_type=jnp.float32
    ).astype(picked_ref.dtype)


def mix_kernel(index_ref, own_ref, edge_ref, arrived_ref, *refs):
    *chunk_refs, mixed_ref, dense_ref, outer_ref = refs
    own = own_ref.shape[0]
    block_rows, chosen = index_ref.shape
    size = own // block_rows
    for b in range(block_rows):
        rows = slice(b * size, (b + 1) * size)
        blocks = [edge_ref[k, rows, :] for k in range(chosen)]
        for j in range(block_rows + outer_ref.shape[1] // size):
            dense = jnp.zeros_like(blocks[0])
            for k in range(chosen):
                here = (index_ref[b : b + 1, k : k + 1] == j).astype(jnp.float32).astype(dense.dtype)
                dense += here * blocks[k]
            if j < block_rows:
                dense_ref[rows, j * size : (j + 1) * size] = dense
            else:
                outer_ref[rows, (j - block_rows) * size : (j - block_rows + 1) * size] = dense
    total = own_ref[...].astype(jnp.float32)
    total += jnp.dot(dense_ref[...], own_ref[...], preferred_element_type=jnp.float32)
    total += jnp.dot(outer_ref[...], arrived_ref[...], preferred_element_type=jnp.float32)
    mixed = total.astype(mixed_ref.dtype)
    mixed_ref[...] = mixed
    at = 0
    for chunk_ref in chunk_refs:
        chunk_ref[...] = mixed[at : at + chunk_ref.shape[0]]
        at += chunk_ref.shape[0]


def stack_kernel(*refs):
    *piece_refs, out_ref, sems = refs
    copies = [pltpu.make_async_copy(ref, out_ref.at[i], sems.at[i]) for i, ref in enumerate(piece_refs)]
    for copy in copies:
        copy.start()
    for copy in copies:
        copy.wait()


def relu_dot(left, right):
    total = jnp.dot(left, right, preferred_element_type=jnp.float32)
    return jnp.maximum(total, 0.0).astype(jnp.bfloat16)


def assemble_kernel(parts, *refs):
    *piece_refs, mine_ref, other_ref, weight_ref, hidden_ref, hidden_other_ref = refs
    _, depth, half = piece_refs[0].shape
    core = lax.rem(lax.axis_index("tm"), CORES)
    part = lax.axis_index("vert")
    around = [lax.rem(part + (parts - 2 * d), parts) for d in range(parts // 2)]
    origin = around + [i ^ 1 for i in around]
    at = 0
    for first, second in zip(piece_refs[::2], piece_refs[1::2]):
        for i in range(first.shape[0]):
            row = pl.ds(pl.multiple_of(origin[at] * depth, depth), depth)
            for ref, side in ((first, core), (second, 1 - core)):
                weight_ref[row, pl.ds(pl.multiple_of(side * half, half), half)] = ref[i]
            at += 1
    hidden_ref[...] = relu_dot(mine_ref[...], weight_ref[...])
    hidden_other_ref[...] = relu_dot(other_ref[...], weight_ref[...])


def arrange_kernel(heads_ref, rows_ref):
    heads, head_rows, _ = heads_ref.shape
    size = head_rows // 3
    for h in range(heads):
        for i in range(3):
            start = (i * heads + h) * size
            rows_ref[start : start + size, :] = heads_ref[h, i * size : (i + 1) * size, :]


def own_kernel(mine_ref, other_ref, rows_ref, query_ref, both_ref, stacked_ref):
    rows = mine_ref.shape[0]
    width = query_ref.shape[2]
    core = lax.rem(lax.axis_index("tm"), CORES)
    stacked_ref[:rows, :] = mine_ref[...]
    stacked_ref[rows:, :] = other_ref[...]
    packed = lax.dot_general(
        stacked_ref[...], rows_ref[...], NT, preferred_element_type=jnp.float32
    ).astype(jnp.bfloat16)
    for t, slot in enumerate((core, 1 - core)):
        part = packed[t * rows : (t + 1) * rows]
        query_ref[slot] = part[:, :width]
        both_ref[slot] = part[:, width:]


def arrange_own_kernel(mine_ref, other_ref, heads_ref, rows_ref, query_ref, both_ref, stacked_ref):
    arrange_kernel(heads_ref, rows_ref)
    own_kernel(mine_ref, other_ref, rows_ref, query_ref, both_ref, stacked_ref)


def attend_kernel(lists, head_size, start, weight_ref, *refs):
    total = sum(lists)
    rows_refs, query_refs, both_refs = refs[:total], refs[total : 2 * total], refs[2 * total : 3 * total]
    *mixed_refs, mine_ref, other_ref, stacked_ref, attended_ref = refs[3 * total :]
    core = lax.rem(lax.axis_index("tm"), CORES)
    chip = lax.div(lax.axis_index("tm"), CORES)
    rows = mine_ref.shape[0]
    here = slice(start, start + rows)
    slot = lambda s: slice(s * rows, (s + 1) * rows)
    for s, ref in enumerate(mixed_refs):
        stacked_ref[slot(s), :] = ref[...]
    raised = relu_dot(stacked_ref[...], weight_ref[...])
    scale = head_size ** (-0.5)
    folded = math.frexp(scale)[0] == 0.5
    at = 0
    for g, count in enumerate(lists):
        members = range(sum(lists[:g]), sum(lists[: g + 1]))
        packed = []
        for m in members:
            first = query_refs[m].shape[2]
            packed.append(lax.dot_general(
                raised, rows_refs[m][first:, :], NT, preferred_element_type=jnp.float32
            ))
        join = lambda parts: jnp.concatenate(parts, axis=1) if len(parts) > 1 else parts[0]
        half = packed[0].shape[1] // 2
        key = join([a[:, :half] for a in packed]).astype(jnp.bfloat16)
        value = join([a[:, half:] for a in packed])
        keys = [key[slot(s)] for s in range(len(mixed_refs))]
        values = [value[slot(s)] for s in range(len(mixed_refs))]
        keys += [join([both_refs[m][u, here, :half] for m in members]) for u in range(CORES)]
        values += [
            join([both_refs[m][u, here, half:] for m in members]).astype(jnp.float32) for u in range(CORES)
        ]
        size = key.shape[1]
        group = lambda axis: lax.broadcasted_iota(jnp.int32, (size, size), axis) // head_size
        spread = jnp.where(group(0) == group(1), scale if folded else 1.0, 0.0).astype(jnp.bfloat16)
        for t in range(CORES):
            slots = len(mixed_refs) + t + 1
            query = join([query_refs[m][t, here, :] for m in members])
            products = jnp.concatenate([query * k for k in keys[:slots]], axis=0)
            scores = jnp.dot(products, spread, preferred_element_type=jnp.float32)
            if not folded:
                scores *= scale
            parts = [scores[slot(u)] for u in range(slots)]
            for u in range(len(mixed_refs)):
                parts[u] = jnp.where(chip >= 1 + u // CORES, parts[u], MASKED)
            top = functools.reduce(jnp.maximum, parts)
            parts = [jnp.exp(part - top) for part in parts]
            result = functools.reduce(jnp.add, [a * b for a, b in zip(parts, values)])
            result *= 1.0 / functools.reduce(jnp.add, parts)
            attended_ref[t, :, at : at + size] = result.astype(attended_ref.dtype)
        at += size
    mine_ref[...] = attended_ref[core]
    other_ref[...] = attended_ref[1 - core]


def combine_kernel(blocks, spots, hidden_ref, *refs):
    *refs, out_ref, sum_ref, sems = refs
    spots = spots(lax.axis_index("tm"), lax.axis_index("vert"))
    pieces = len(spots) // CORES
    width = refs[0].shape[1] // pieces
    lanes = width % LANES == 0
    step = math.gcd(*[ref.shape[0] for ref in refs])
    copies = []
    at = 0
    for r in range(blocks):
        for first in range(0, refs[r].shape[0], step):
            rows = slice(first, first + step)
            here = slice(at, at + step)
            whole = None if lanes else hidden_ref[here, :].astype(jnp.float32)
            for half in range(CORES):
                for p in range(pieces):
                    start = spots[half * pieces + p] * width
                    attended = refs[half * blocks + r][rows, p * width : (p + 1) * width]
                    if lanes:
                        column = pl.ds(pl.multiple_of(start, width), width)
                        total = hidden_ref[here, column].astype(jnp.float32) + attended.astype(jnp.float32)
                        sum_ref[here, column] = total.astype(sum_ref.dtype)
                    else:
                        shape = (width, out_ref.shape[1])
                        spot = lax.broadcasted_iota(jnp.int32, shape, 0) + start
                        spot = (spot == lax.broadcasted_iota(jnp.int32, shape, 1)).astype(jnp.bfloat16)
                        whole += jnp.dot(attended, spot, preferred_element_type=jnp.float32)
            if not lanes:
                sum_ref[here, :] = whole.astype(sum_ref.dtype)
            copies.append(pltpu.make_async_copy(sum_ref.at[here], out_ref.at[here], sems.at[len(copies)]))
            copies[-1].start()
            at += step
    for copy in copies:
        copy.wait()


def shards(sizes, features, graph_weight, head_weight, send_rows, send_count, block_index, block_values):
    steps, parts = sizes["tm"], sizes["vert"]
    chips = steps // CORES
    step, part = lax.axis_index("tm"), lax.axis_index("vert")
    core, chip = step % CORES, step // CORES
    swap_core = lambda a: lax.ppermute(a, "tm", [(i, i ^ 1) for i in range(steps)])
    swap_part = lambda a, bit: lax.ppermute(a, "vert", [(i, i ^ bit) for i in range(parts)])
    turn = lambda a, axis, by, n: lax.ppermute(a, axis, [(i, (i + by) % n) for i in range(n)])
    heads, head_rows, _ = head_weight.shape
    shared = heads % 2 == 0 and parts % 4 == 0
    shares = 2 if shared else 1
    share = (part >> 1) % shares

    def spots(step, part):
        share = lax.rem(lax.div(part, 2), shares)
        places = [step * shares + i for i in range(shares)]
        for d in range(1, chips):
            block = lax.rem(step + (steps - CORES * d), steps) * shares
            places += [block + share, block + 1 - share] if shared else [block]
        return places + [i ^ shares for i in places]

    inputs = features[0]
    own, width = inputs.shape

    head_size = head_rows // 3
    sent = lax.dynamic_slice_in_dim(head_weight, share * (heads // shares), heads // shares, 0)
    fetched = [turn(sent, "tm", CORES * d, steps) for d in range(1, chips)]

    rows_list = send_rows[0, 0]
    sources, most_rows = rows_list.shape
    live = jnp.arange(most_rows)[None, :] < send_count[0, 0][:, None]
    slots = jnp.where(live, rows_list, -1).reshape(1, -1)
    picked = call(
        pick_kernel, shaped(sources * most_rows, width), (slots, inputs),
        specs=[VMEM, VMEM], grid=(), flops=2 * own * width * sources * most_rows,
    )
    arrived = lax.all_to_all(
        picked.reshape(sources, most_rows, width), "vert", split_axis=0, concat_axis=0, tiled=True
    ).reshape(picked.shape)

    depth = graph_weight.shape[0]
    half = width // CORES
    piece = lax.dynamic_slice(graph_weight, (0, core * half), (depth, half))
    around = [turn(piece, "vert", 2 * d, parts) for d in range(1, parts // 2)]
    around = call(
        stack_kernel, shaped(parts // 2, depth, half), (piece, *around),
        specs=[ANY] * (parts // 2), grid=(), limit=16, seconds=4e-6,
        scratch=[pltpu.SemaphoreType.DMA((parts // 2,))],
    )
    across = swap_part(around, 1)

    cuts = [own * cut // ROW_CUTS[-1] for cut in ROW_CUTS]
    blocks = len(cuts) - 1
    outer_size = sources * most_rows
    *chunks, mixed = call(
        mix_kernel,
        (*[shaped(b - a, width) for a, b in zip(cuts, cuts[1:])], shaped(own, width)),
        (block_index[0], inputs, block_values[0].transpose(1, 0, 2), arrived),
        specs=[VMEM] * 4, grid=(),
        scratch=[pltpu.VMEM((own, own), jnp.bfloat16), pltpu.VMEM((own, outer_size), jnp.bfloat16)],
    )
    lower = [
        [
            turn(chunk, "tm", CORES * d, steps)
            for d in range(1, chips)
        ]
        for chunk in chunks
    ]
    arranged = call(arrange_kernel, shaped(heads * head_rows, width), (after(head_weight, mixed),))
    across = after(across, arranged)
    groups = [[group, swap_part(group, 2)] if shared else [group] for group in fetched]
    weight, hidden, sibling = call(
        functools.partial(assemble_kernel, parts),
        (shaped(width, width), shaped(own, width), shaped(own, width)),
        (
            around, swap_core(around), across, swap_core(across), mixed, swap_core(mixed),
        ),
        flops=4 * own * width * width,
    )

    def place(weights, ready=None, seconds=0):
        count = weights.shape[0] // 3 if ready else weights.shape[0] * head_size
        outs = (shaped(CORES, own, count), shaped(CORES, own, 2 * count))
        if not ready:
            outs = (shaped(3 * count, width), *outs)
        result = call(
            own_kernel if ready else arrange_own_kernel,
            outs,
            (hidden, sibling, weights),
            seconds=seconds,
            scratch=[pltpu.VMEM((CORES * own, width), jnp.bfloat16)],
        )
        return (weights, *result) if ready else result

    owned = [place(arranged, True)]
    for group in groups:
        group = list(group)
        for i, weights in enumerate(group):
            if i == len(group) - 1:
                owned, lower[0], weights = lax.optimization_barrier((owned, lower[0], weights))
            owned.append(place(weights, seconds=12e-6 if i == len(group) - 1 else 0))
    lists = [1, *[len(group) for group in groups]]

    total = chips * heads * head_size
    kept, got = [], []
    token = owned[0][1]
    for r in range(blocks):
        rows = cuts[r + 1] - cuts[r]
        chunk = after(lower[r], token)
        mixed_rows = [a for b in chunk for a in (b, swap_core(b))]
        keep, send = token = call(
            functools.partial(attend_kernel, lists, head_size, cuts[r]),
            (shaped(rows, total), shaped(rows, total)),
            (weight, *[a[i] for i in range(3) for a in owned], *mixed_rows),
            limit=11 + len(mixed_rows) * rows * width // 2**17,
            flops=2 * len(mixed_rows) * rows * width * (2 * total + width),
            scratch=[
                pltpu.VMEM((len(mixed_rows) * rows, width), jnp.bfloat16),
                pltpu.VMEM((CORES, rows, total), jnp.bfloat16),
            ],
        )
        kept.append(keep)
        got.append(swap_core(send))
    combined = call(
        functools.partial(combine_kernel, blocks, spots),
        shaped(own, width),
        (hidden, *kept, *got),
        out_specs=ANY,
        scratch=[
            pltpu.VMEM((own, width), jnp.bfloat16),
            pltpu.SemaphoreType.DMA((own // math.gcd(*[a.shape[0] for a in kept]),)),
        ],
    )
    return combined[None]


def solution(mesh):
    return jax.shard_map(
        functools.partial(shards, dict(mesh.shape)),
        mesh=mesh,
        in_specs=(
            P("tm", "vert", None),
            P("vert", None),
            P("tm", None, None),
            P("tm", "vert", None, None),
            P("tm", "vert", None),
            P("tm", "vert", None),
            P("tm", "vert", None, None),
        ),
        out_specs=P("tm", "vert", None),
        check_vma=False,
    )
```
